512 devices in a mesh: dp: 64 (over x, z_lo, core), tensor: 8 (over z_hi, y).
Axes of the slice: x: 4, y: 4, z: 16 (z_hi: 2, z_lo: 8; z = z_hi * 8 + z_lo), core: 2. Of those that a mesh axis runs over, the one named last changes fastest.
Arguments:
- query_heads: bfloat16 [32768, 8192], P('dp', 'tensor'), may hold values from -165 to 165
- key_heads: bfloat16 [32768, 1024], P('dp', 'tensor'), may hold values from -6 to 6
- value_heads: bfloat16 [32768, 1024], P('dp', 'tensor'), may hold values from -6 to 6
- logp_grad: bfloat16 [32768, 8192], P('dp', 'tensor'), may hold values from -6 to 6
- logp_new: float32 [32768], P(('dp', 'tensor')), may hold values from -3 to 0
- logp_old: float32 [32768], P(('dp', 'tensor')), may hold values from -3 to 0
- advantage: float32 [32768], P(('dp', 'tensor')), may hold values from -6 to 6
- ratio_caps: float32 [4], replicated, may hold values from 1.05 to 2
- live_counts: int32 [64], P('dp'), may hold values from 0 to 512, as said below
- seq_begin: int32 [32768], P('dp'), may hold values from 0 to 511, as said below
- seg_begin: int32 [32768], P('dp'), may hold values from 0 to 511, as said below
- policy_version: int32 [32768], P('dp'), may hold values from 0 to 3, as said below
Outputs:
- grad_queries: bfloat16 [32768, 8192], P('dp', 'tensor')
- grad_keys: bfloat16 [32768, 1024], P('dp', 'tensor')
- grad_values: bfloat16 [32768, 1024], P('dp', 'tensor')
The draws below stay inside these ranges and needn't reach their ends.
Inputs may be any that keep to these rules, and one draw needn't show every extreme that they name: `live_counts`: rows of a block from its count on are padding. `seq_begin`: given as a row of the block (0 to 511); each sequence is a run of consecutive rows that begins at that row; every padding row is a sequence of its own. `seg_begin`: given as a row of the block; segments are runs of consecutive rows inside one sequence, and every sequence begins a segment. `policy_version`: all rows of a segment share one version.
All inputs are finite; a program needn't handle non-finite values.
Results may differ from the reference program's by a relative error of at most 0.017.
Values may be sent and summed in bfloat16 or wider, within the bound.
A program may use at most 64 MiB of HBM per device.

```python
import math
import jax
import jax.numpy as jnp
from jax import lax

HEADS = 64
KV_HEADS = 8
HEAD_DIM = 128
ROWS = 512
VERSIONS = 4
TOKENS = 32768
N_DP = 64


def layout(key):
    key = jax.random.fold_in(key, 101)
    count_key, full_key, seq_key, seg_key, version_key = jax.random.split(key, 5)
    device_rank = jnp.arange(N_DP, dtype=jnp.int32)
    ramp_base = ROWS // 16 + device_rank * (3 * ROWS // 4) // max(N_DP - 1, 1)
    counts = ramp_base + jax.random.randint(count_key, (N_DP,), 0, ROWS // 8 + 1)
    full_device = jax.random.randint(full_key, (), 0, N_DP)
    counts = jnp.where(device_rank == full_device, ROWS, counts).astype(jnp.int32)
    positions = jnp.arange(ROWS, dtype=jnp.int32)
    live_rows = positions[None, :] < counts[:, None]
    seq_draw = jax.random.randint(seq_key, (N_DP, ROWS), 0, max(ROWS // 16, 2))
    seq_mark = (seq_draw == 0) | (positions[None, :] == 0) | jnp.logical_not(live_rows)
    starts = lax.cummax(jnp.where(seq_mark, positions[None, :], 0), axis=1)
    seg_draw = jax.random.randint(seg_key, (N_DP, ROWS), 0, 16)
    seg_mark = seq_mark | (seg_draw == 0)
    seg_starts = lax.cummax(jnp.where(seg_mark, positions[None, :], 0), axis=1)
    version_draw = jax.random.randint(version_key, (N_DP, ROWS), 0, VERSIONS)
    versions = jnp.take_along_axis(version_draw, seg_starts, axis=1)
    return (counts, starts.reshape(TOKENS).astype(jnp.int32), seg_starts.reshape(TOKENS).astype(jnp.int32), versions.reshape(TOKENS).astype(jnp.int32), live_rows.reshape(TOKENS))


def key_base(key):
    key = jax.random.fold_in(key, 202)
    return jnp.clip(jax.random.normal(key, (TOKENS, KV_HEADS * HEAD_DIM), jnp.float32), -6.0, 6.0)


def draw_query_heads(key, part):
    key = jax.random.fold_in(key, 11)
    queries = jnp.clip(jax.random.normal(key, (TOKENS, HEADS * HEAD_DIM), jnp.float32), -6.0, 6.0)
    return queries.astype(jnp.bfloat16)


def draw_key_heads(key, part):
    base_keys = key_base(key)
    result = base_keys
    return result.astype(jnp.bfloat16)


def draw_live_counts(key, part):
    shared = layout(key)
    return shared[0]


def draw_seq_begin(key, part):
    shared = layout(key)
    return shared[1]


def draw_seg_begin(key, part):
    shared = layout(key)
    return shared[2]


def draw_policy_version(key, part):
    shared = layout(key)
    return shared[3]


def levels(own_key, extent, cuts, low, largest):
    def one(axis_at, shards_of):
        heights = jax.random.uniform(jax.random.fold_in(jax.random.fold_in(own_key, 6), axis_at), (shards_of,), jnp.float32, low / len(cuts), largest / len(cuts))
        return jnp.repeat(jnp.exp(heights), extent[axis_at] // shards_of).reshape((-1,) + (1,) * (len(extent) - axis_at - 1))

    level = one(*cuts[0])
    for cut in cuts[1:]:
        level = level * one(*cut)
    return level


def noise(stream_key, shape, deviation, limit, shards=(), kind=jnp.bfloat16):
    values = jax.random.normal(stream_key, shape, jnp.float32) * deviation
    if len(shards) > 0:
        values = levels(stream_key, shape, shards, -0.22, 0.18) * values
    return jnp.clip(values, min=-limit, max=limit).astype(kind)


def setup_inputs(seed: int = 0) -> dict:
    streams_of = jax.random.split(jax.random.key(seed), 13)
    query_heads = draw_query_heads(jax.random.fold_in(streams_of[12], 71), 0)
    key_heads = draw_key_heads(jax.random.fold_in(streams_of[12], 71), 0)
    value_heads = noise(streams_of[2], (TOKENS, KV_HEADS * HEAD_DIM), 1.0, 6.0, ((0, 64), (1, 8)))
    logp_grad = noise(streams_of[3], (TOKENS, HEADS * HEAD_DIM), 1.0, 6.0, ((0, 64), (1, 8)))
    logp_new = jnp.clip(-3.0 + 3.0 * jax.random.uniform(streams_of[4], (TOKENS,), jnp.float32) ** levels(streams_of[4], (TOKENS,), ((0, 512),), -0.2, 0.2), -3.0, 0.0)
    logp_old = jnp.clip(-3.0 + 3.0 * jax.random.uniform(streams_of[5], (TOKENS,), jnp.float32) ** levels(streams_of[5], (TOKENS,), ((0, 512),), -0.2, 0.2), -3.0, 0.0)
    advantage = noise(streams_of[6], (TOKENS,), 1.0, 6.0, ((0, 512),), jnp.float32)
    ratio_caps = jnp.clip(jnp.exp(jax.random.uniform(streams_of[7], (VERSIONS,), jnp.float32, math.log(1.05), math.log(2.0))), 1.05, 2.0)
    live_counts = draw_live_counts(jax.random.fold_in(streams_of[12], 71), 0)
    seq_begin = draw_seq_begin(jax.random.fold_in(streams_of[12], 71), 0)
    seg_begin = draw_seg_begin(jax.random.fold_in(streams_of[12], 71), 0)
    policy_version = draw_policy_version(jax.random.fold_in(streams_of[12], 71), 0)
    return {"query_heads": query_heads, "key_heads": key_heads, "value_heads": value_heads, "logp_grad": logp_grad, "logp_new": logp_new, "logp_old": logp_old, "advantage": advantage, "ratio_caps": ratio_caps, "live_counts": live_counts, "seq_begin": seq_begin, "seg_begin": seg_begin, "policy_version": policy_version}


def block_backward(block):
    query_block, key_block, value_block, dout_block, begin_block = block
    positions = jnp.arange(ROWS, dtype=jnp.int32)
    groups = HEADS // KV_HEADS
    score_scale = HEAD_DIM ** -0.5
    allowed = (positions[None, :] >= begin_block[:, None]) & (positions[None, :] <= positions[:, None])
    q_float = query_block.astype(jnp.float32).reshape(ROWS, KV_HEADS, groups, HEAD_DIM)
    d_float = dout_block.astype(jnp.float32).reshape(ROWS, KV_HEADS, groups, HEAD_DIM)
    k_float = key_block.astype(jnp.float32).reshape(ROWS, KV_HEADS, HEAD_DIM)
    v_float = value_block.astype(jnp.float32).reshape(ROWS, KV_HEADS, HEAD_DIM)
    scores = jnp.einsum("tkgd,jkd->kgtj", q_float, k_float) * score_scale
    scores = jnp.where(allowed, scores, -jnp.inf)
    row_top = jnp.max(scores, axis=-1, keepdims=True)
    log_norm = row_top + jnp.log(jnp.sum(jnp.exp(scores - row_top), axis=-1, keepdims=True))
    probs = jnp.exp(scores - log_norm)
    d_prob = jnp.einsum("tkgd,jkd->kgtj", d_float, v_float)
    row_delta = jnp.sum(probs * d_prob, axis=-1, keepdims=True)
    d_score = (probs * (d_prob - row_delta)).astype(jnp.bfloat16).astype(jnp.float32)
    probs_b = probs.astype(jnp.bfloat16).astype(jnp.float32)
    grad_v = jnp.einsum("kgtj,tkgd->jkd", probs_b, d_float)
    grad_k = jnp.einsum("kgtj,tkgd->jkd", d_score, q_float) * score_scale
    grad_q = jnp.einsum("kgtj,jkd->tkgd", d_score, k_float) * score_scale
    return (grad_q.reshape(ROWS, HEADS * HEAD_DIM).astype(jnp.bfloat16),
            grad_k.reshape(ROWS, KV_HEADS * HEAD_DIM).astype(jnp.bfloat16),
            grad_v.reshape(ROWS, KV_HEADS * HEAD_DIM).astype(jnp.bfloat16))


def reference(query_heads, key_heads, value_heads, logp_grad, logp_new, logp_old, advantage, ratio_caps, live_counts, seq_begin, seg_begin, policy_version):
    positions = jnp.arange(ROWS, dtype=jnp.int32)
    live_rows = positions[None, :] < live_counts[:, None]
    live_total = jnp.sum(live_counts.astype(jnp.float32))
    log_ratio = (logp_new - logp_old).reshape(N_DP, ROWS)
    segments = seg_begin.reshape(N_DP, ROWS)
    same_seg = segments[:, :, None] == segments[:, None, :]
    seg_sum = jnp.sum(jnp.where(same_seg, log_ratio[:, None, :], 0.0), axis=2)
    seg_len = jnp.sum(same_seg.astype(jnp.float32), axis=2)
    weight = jnp.minimum(jnp.exp(seg_sum / seg_len), ratio_caps[policy_version.reshape(N_DP, ROWS)])
    loss_coef = jnp.where(live_rows, -advantage.reshape(N_DP, ROWS) * weight * (TOKENS / live_total), 0.0)
    d_out = (loss_coef[:, :, None] * logp_grad.reshape(N_DP, ROWS, HEADS * HEAD_DIM).astype(jnp.float32)).astype(jnp.bfloat16)
    grads = lax.map(block_backward, (query_heads.reshape(N_DP, ROWS, HEADS * HEAD_DIM),
                                     key_heads.reshape(N_DP, ROWS, KV_HEADS * HEAD_DIM),
                                     value_heads.reshape(N_DP, ROWS, KV_HEADS * HEAD_DIM),
                                     d_out, seq_begin.reshape(N_DP, ROWS)))
    return (grads[0].reshape(TOKENS, HEADS * HEAD_DIM),
            grads[1].reshape(TOKENS, KV_HEADS * HEAD_DIM),
            grads[2].reshape(TOKENS, KV_HEADS * HEAD_DIM))
```

```python
import functools
import math

import jax
import jax.numpy as jnp
from jax import lax
from jax.experimental import pallas as pl
from jax.experimental.pallas import tpu as pltpu
from jax.sharding import PartitionSpec as P

HEAD_DIM = 128
TILE = 128
MESH = pl.DeviceIdType.MESH
NEG = -1e30


def in_hbm(*arrays):
    return [pltpu.with_memory_space_constraint(a, pltpu.HBM) for a in arrays]


def flips(index, bits):
    return [(1 << b) * (1 - 2 * lax.rem(lax.div(index, 1 << b), 2)) for b in bits]


def partners(index, bits):
    deltas = flips(index, bits)
    found = []
    for mask in range(1, 1 << len(bits)):
        other = index
        for n, delta in enumerate(deltas):
            if mask >> n & 1:
                other = other + delta
        found.append(other)
    return found


def exchange_kernel(plane_bits, line_bits, nt, new_hbm, old_hbm, adv_hbm, cnt_s, gath_ref, total_ref,
                    new_v, old_v, adv_v, own_row, rows, cnt_row, cnt_rows, part_row, part_rows,
                    load_sem, send_sem, recv_sem):
    dp = lax.axis_index("dp")
    me = lax.axis_index("tensor")
    owners = partners(me, range(nt.bit_length() - 1))
    tensor_peers = [(dp, t) for t in owners]
    plane_peers = [(d, me) for d in partners(dp, plane_bits)]
    line_peers = [(d, me) for d in partners(dp, line_bits)]
    planes, nz = len(plane_peers) + 1, len(line_peers) + 1
    peers = tensor_peers + plane_peers + line_peers

    barrier = pltpu.get_barrier_semaphore()
    for peer in peers:
        pl.semaphore_signal(barrier, inc=1, device_id=peer, device_id_type=MESH)
    loads = [
        pltpu.make_async_copy(src, dst, load_sem.at[n])
        for n, (src, dst) in enumerate(
            ((new_hbm, new_v), (old_hbm, old_v), (adv_hbm, adv_v)))
    ]
    for load in loads:
        load.start()
    for load in loads:
        load.wait()
    own_row[0] = jnp.concatenate([new_v[...] - old_v[...], adv_v[...]], axis=1)
    cnt_row[0] = jnp.full((1, 128), cnt_s[0].astype(jnp.float32), jnp.float32)
    pl.semaphore_wait(barrier, len(peers))

    def send(src, dst, n, peer):
        pltpu.make_async_remote_copy(
            src_ref=src, dst_ref=dst, send_sem=send_sem.at[n], recv_sem=recv_sem.at[n],
            device_id=peer, device_id_type=MESH).start()

    def drain(buffer, n, sem):
        span = buffer.at[pl.ds(0, n)]
        pltpu.make_async_copy(span, span, sem).wait()

    for step in range(1, planes):
        send(cnt_row, cnt_rows.at[pl.ds(step - 1, 1)], 0, plane_peers[step - 1])
    for step in range(1, nt):
        send(own_row, rows.at[pl.ds(step - 1, 1)], 1, tensor_peers[step - 1])
    drain(cnt_rows, planes - 1, recv_sem.at[0])
    part = cnt_row[0]
    for n in range(planes - 1):
        part = part + cnt_rows[n]
    part_row[0] = part
    for step in range(1, nz):
        send(part_row, part_rows.at[pl.ds(step - 1, 1)], 2, line_peers[step - 1])
    drain(rows, nt - 1, recv_sem.at[1])
    owner_row = lax.broadcasted_iota(jnp.int32, (nt, 128), 0)
    gathered = jnp.broadcast_to(own_row[0], (nt, 128))
    for n in range(nt - 1):
        gathered = jnp.where(owner_row == owners[n], jnp.broadcast_to(rows[n], (nt, 128)), gathered)
    gath_ref[...] = gathered
    drain(part_rows, nz - 1, recv_sem.at[2])
    total = part
    for n in range(nz - 1):
        total = total + part_rows[n]
    total_ref[...] = total
    drain(cnt_rows, planes - 1, send_sem.at[0])
    drain(rows, nt - 1, send_sem.at[1])
    drain(part_rows, nz - 1, send_sem.at[2])


def exchange(sizes, logp_new, logp_old, advantage, live_counts):
    plane_bits, line_bits, nt = sizes
    planes, nz = 1 << len(plane_bits), 1 << len(line_bits)
    own = logp_new.shape[0]
    f32 = jnp.float32
    any_spec = pl.BlockSpec(memory_space=pltpu.HBM)
    vmem = pl.BlockSpec(memory_space=pltpu.VMEM)
    return pl.pallas_call(
        functools.partial(exchange_kernel, plane_bits, line_bits, nt),
        out_shape=(jax.ShapeDtypeStruct((nt, 128), f32), jax.ShapeDtypeStruct((1, 128), f32)),
        in_specs=[any_spec] * 3 + [pl.BlockSpec(memory_space=pltpu.SMEM)],
        out_specs=(vmem, vmem),
        scratch_shapes=[
            pltpu.VMEM((1, own), f32),
            pltpu.VMEM((1, own), f32),
            pltpu.VMEM((1, own), f32),
            pltpu.VMEM((1, 1, 128), f32),
            pltpu.VMEM((nt - 1, 1, 128), f32),
            pltpu.VMEM((1, 1, 128), f32),
            pltpu.VMEM((planes - 1, 1, 128), f32),
            pltpu.VMEM((1, 1, 128), f32),
            pltpu.VMEM((nz - 1, 1, 128), f32),
            pltpu.SemaphoreType.DMA((4,)),
            pltpu.SemaphoreType.DMA((3,)),
            pltpu.SemaphoreType.DMA((3,)),
        ],
        compiler_params=pltpu.CompilerParams(collective_id=0, has_side_effects=True),
        name="exchange",
    )(*in_hbm(logp_new.reshape(1, own), logp_old.reshape(1, own), advantage.reshape(1, own)), live_counts)


def row_coefs(tokens, gath, total, seg_row, ver_row, caps, count):
    nt = gath.shape[0]
    rows = seg_row.shape[1]
    half = rows // nt
    bf16, f32 = jnp.bfloat16, jnp.float32
    lane = lax.broadcasted_iota(jnp.int32, (nt, 128), 1)
    other = pltpu.roll(gath, half, 1)
    ratio = jnp.where(lane < half, gath, other)
    adv = jnp.where(lane < half, other, gath)
    place = lax.broadcasted_iota(jnp.int32, (nt, rows), 1) // half
    mine = place == lax.broadcasted_iota(jnp.int32, (nt, rows), 0)
    copies = rows // 128
    ratio = jnp.where(mine, jnp.concatenate([ratio] * copies, axis=1), 0.0)
    adv = jnp.sum(jnp.where(mine, jnp.concatenate([adv] * copies, axis=1), 0.0), axis=0, keepdims=True)
    hi = ratio.astype(bf16).astype(f32)
    mid = (ratio - hi).astype(bf16).astype(f32)
    low = ratio - hi - mid
    ones = jnp.ones((nt, rows), f32)
    left = jnp.concatenate([hi, mid, low, ones], axis=0).astype(bf16)
    seg = seg_row.astype(f32)
    seg_col = jnp.broadcast_to(seg, (128, rows)).T
    sums = []
    for a in range(rows // 128):
        same = jnp.where(seg_col == seg[:, a * 128:(a + 1) * 128], 1.0, 0.0).astype(bf16)
        sums.append(jnp.dot(left, same, preferred_element_type=f32))
    sums = jnp.concatenate(sums, axis=1)
    seg_sum = jnp.sum(sums[:3 * nt], axis=0, keepdims=True)
    seg_len = sums[3 * nt:3 * nt + 1]
    cap = jnp.zeros((1, rows), f32)
    for n in range(caps.shape[0]):
        cap = jnp.where(ver_row == n, caps[n], cap)
    weight = jnp.minimum(jnp.exp(seg_sum / seg_len), cap)
    total = jnp.concatenate([total] * copies, axis=1)
    live = lax.broadcasted_iota(jnp.int32, (1, rows), 1) < count
    return jnp.where(live, -adv * weight * (tokens / total), 0.0)


def attend_kernel(tokens, cnt_s, gath_ref, total_ref, seq_hbm, caps_hbm, seq_row_hbm, seg_hbm, ver_hbm,
                  q_hbm, k_hbm, v_hbm, g_hbm, dq_hbm, dk_hbm, dv_hbm,
                  q, k, v, g, dq, dk, dv, probs_t, dscore_t, k_t, bias,
                  seq_s, caps_s, seq_ref, seg_ref, ver_ref, sems):
    rows, columns = q.shape
    heads = columns // HEAD_DIM
    tiles = rows // TILE
    bf16, f32 = jnp.bfloat16, jnp.float32
    scale = HEAD_DIM ** -0.5
    factor = scale * math.log2(math.e)

    def tile_rows(i):
        return pl.ds(i * TILE, TILE)

    k_in = pltpu.make_async_copy(k_hbm, k, sems.at[0])
    v_in = pltpu.make_async_copy(v_hbm, v, sems.at[1])
    q_in = [pltpu.make_async_copy(q_hbm.at[tile_rows(i)], q.at[tile_rows(i)], sems.at[2 + i]) for i in range(tiles)]
    g_in = [pltpu.make_async_copy(g_hbm.at[tile_rows(i)], g.at[tile_rows(i)], sems.at[2 + tiles + i])
            for i in range(tiles)]
    dq_out = [pltpu.make_async_copy(dq.at[tile_rows(i)], dq_hbm.at[tile_rows(i)], sems.at[2 + 2 * tiles + i])
              for i in range(tiles)]
    dv_out = pltpu.make_async_copy(dv, dv_hbm, sems.at[2 + 3 * tiles])
    dk_out = pltpu.make_async_copy(dk, dk_hbm, sems.at[3 + 3 * tiles])
    small = [
        pltpu.make_async_copy(src, dst, sems.at[4 + 3 * tiles + n])
        for n, (src, dst) in enumerate(((seq_hbm, seq_s), (caps_hbm, caps_s),
                                        (seq_row_hbm, seq_ref), (seg_hbm, seg_ref), (ver_hbm, ver_ref)))
    ]
    for load in small:
        load.start()
    k_in.start()
    v_in.start()
    for i in range(tiles):
        q_in[i].start()
        g_in[i].start()
    for load in small:
        load.wait()
    coef = row_coefs(tokens, gath_ref[...], total_ref[...], seg_ref[...], ver_ref[...], caps_s, cnt_s[0])
    k_in.wait()
    v_in.wait()
    k_t[...] = k[...].astype(f32).T.astype(bf16)

    def head_pair(ref, i, p):
        return jnp.concatenate(
            [ref[i * TILE:(i + 1) * TILE, (2 * p + n) * HEAD_DIM:(2 * p + n + 1) * HEAD_DIM] for n in range(2)],
            axis=0)

    contract_last = (((1,), (1,)), ((), ()))

    def body(first):
        for i in range(tiles):
            j0, j1 = first[i] * TILE, (i + 1) * TILE
            span = j1 - j0
            row_j = lax.broadcasted_iota(jnp.int32, (span, TILE), 0) + j0
            col_t = lax.broadcasted_iota(jnp.int32, (span, TILE), 1) + i * TILE
            begin = seq_ref[:, i * TILE:(i + 1) * TILE]
            bias[0:span, :] = jnp.where((row_j >= begin) & (row_j <= col_t), 0.0, NEG)
            q_in[i].wait()
            g_in[i].wait()
            coef_i = coef[:, i * TILE:(i + 1) * TILE]
            coef_pair = jnp.concatenate([coef_i, coef_i], axis=1)
            for p in range(heads // 2):
                scores = lax.dot_general(k[j0:j1, :], head_pair(q, i, p), contract_last, preferred_element_type=f32)
                d_prob = lax.dot_general(v[j0:j1, :], head_pair(g, i, p), contract_last, preferred_element_type=f32)
                scores = scores + jnp.concatenate([bias[0:span, :]] * 2, axis=1)
                top = jnp.max(scores, axis=0, keepdims=True)
                mass = jnp.exp2((scores - top) * factor)
                norm = 1.0 / jnp.sum(mass, axis=0, keepdims=True)
                delta = jnp.sum(mass * d_prob, axis=0, keepdims=True) * norm
                weighted = mass * (norm * coef_pair)
                lanes = slice(i * columns + 2 * p * TILE, i * columns + 2 * (p + 1) * TILE)
                probs_t[j0:j1, lanes] = weighted.astype(bf16)
                dscore_t[j0:j1, lanes] = (weighted * (d_prob - delta)).astype(bf16)
            dq_t = jnp.dot(k_t[:, j0:j1], dscore_t[j0:j1, i * columns:(i + 1) * columns],
                           preferred_element_type=f32) * scale
            for h in range(heads):
                dq[i * TILE:(i + 1) * TILE, h * HEAD_DIM:(h + 1) * HEAD_DIM] = (
                    dq_t[:, h * TILE:(h + 1) * TILE].T.astype(bf16))
            dq_out[i].start()
        for j in range(tiles):
            users = [i for i in range(j, tiles) if first[i] <= j]
            lanes = slice(users[0] * columns, (users[-1] + 1) * columns)
            stack = [(i, h) for i in users for h in range(heads)]
            for source, right, target, factor_out in ((probs_t, g, dv, None), (dscore_t, q, dk, scale)):
                stacked = jnp.concatenate(
                    [right[i * TILE:(i + 1) * TILE, h * HEAD_DIM:(h + 1) * HEAD_DIM] for i, h in stack], axis=0)
                value = jnp.dot(source[j * TILE:(j + 1) * TILE, lanes], stacked, preferred_element_type=f32)
                if factor_out is not None:
                    value = value * factor_out
                target[j * TILE:(j + 1) * TILE, :] = value.astype(bf16)

    dense = [0] * tiles
    band = [max(i - 1, 0) for i in range(tiles)]
    near = seq_s[0] >= 0
    for i in range(2, tiles):
        near = near & (seq_s[i * TILE] >= band[i] * TILE)

    @pl.when(near)
    def _():
        body(band)

    @pl.when(jnp.logical_not(near))
    def _():
        body(dense)

    dv_out.start()
    dk_out.start()
    for i in range(tiles):
        dq_out[i].wait()
    dv_out.wait()
    dk_out.wait()


def attend(tokens, gath, total, ratio_caps, live_counts, seq_begin, seg_begin, policy_version, q, k, v, g):
    rows, columns = q.shape
    tiles = rows // TILE
    bf16 = jnp.bfloat16
    vmem = pl.BlockSpec(memory_space=pltpu.VMEM)
    any_spec = pl.BlockSpec(memory_space=pltpu.HBM)
    wide, narrow = (rows, columns), (rows, HEAD_DIM)
    return pl.pallas_call(
        functools.partial(attend_kernel, tokens),
        out_shape=tuple(jax.ShapeDtypeStruct(s, bf16) for s in (wide, narrow, narrow)),
        in_specs=[pl.BlockSpec(memory_space=pltpu.SMEM)] + [vmem] * 2 + [any_spec] * 9,
        out_specs=(any_spec,) * 3,
        scratch_shapes=[
            pltpu.VMEM(wide, bf16),
            pltpu.VMEM(narrow, bf16),
            pltpu.VMEM(narrow, bf16),
            pltpu.VMEM(wide, bf16),
            pltpu.VMEM(wide, bf16),
            pltpu.VMEM(narrow, bf16),
            pltpu.VMEM(narrow, bf16),
            pltpu.VMEM((rows, tiles * columns), bf16),
            pltpu.VMEM((rows, tiles * columns), bf16),
            pltpu.VMEM((HEAD_DIM, rows), bf16),
            pltpu.VMEM((rows, TILE), jnp.float32),
            pltpu.SMEM((rows,), jnp.int32),
            pltpu.SMEM(ratio_caps.shape, jnp.float32),
            pltpu.VMEM((1, rows), jnp.int32),
            pltpu.VMEM((1, rows), jnp.int32),
            pltpu.VMEM((1, rows), jnp.int32),
            pltpu.SemaphoreType.DMA((10 + 3 * tiles,)),
        ],
        compiler_params=pltpu.CompilerParams(vmem_limit_bytes=40 * 2**20),
        name="attend",
    )(live_counts, gath, total, *in_hbm(seq_begin, ratio_caps, seq_begin.reshape(1, rows), seg_begin.reshape(1, rows),
                           policy_version.reshape(1, rows), q, k, v, g))


def solution(mesh):
    blocks, nt = mesh.shape["dp"], mesh.shape["tensor"]
    top = blocks.bit_length() - 1
    plane_bits, line_bits = (0, top - 2, top - 1), tuple(range(1, top - 2))

    def local(query_heads, key_heads, value_heads, logp_grad, logp_new, logp_old, advantage, ratio_caps,
              live_counts, seq_begin, seg_begin, policy_version):
        tokens = float(query_heads.shape[0] * blocks)
        gath, total = exchange((plane_bits, line_bits, nt), logp_new, logp_old, advantage, live_counts)
        return attend(tokens, gath, total, ratio_caps, live_counts, seq_begin, seg_begin, policy_version,
                      query_heads, key_heads, value_heads, logp_grad)

    row, every = P("dp"), P(("dp", "tensor"))
    both = P("dp", "tensor")
    return jax.shard_map(
        local,
        mesh=mesh,
        in_specs=(both, both, both, both, every, every, every, P(), row, row, row, row),
        out_specs=(both, both, both),
        check_vma=False,
    )
```

```python
import functools
import math

import jax
import jax.numpy as jnp
from jax import lax
from jax.experimental import pallas as pl
from jax.experimental.pallas import tpu as pltpu
from jax.sharding import PartitionSpec as P

HEAD_DIM = 128
TILE = 128
MESH = pl.DeviceIdType.MESH
NEG = -1e30


def in_hbm(*arrays):
    return [pltpu.with_memory_space_constraint(a, pltpu.HBM) for a in arrays]


def flips(index, bits):
    return [(1 << b) * (1 - 2 * lax.rem(lax.div(index, 1 << b), 2)) for b in bits]


def partners(index, bits):
    deltas = flips(index, bits)
    found = []
    for mask in range(1, 1 << len(bits)):
        other = index
        for n, delta in enumerate(deltas):
            if mask >> n & 1:
                other = other + delta
        found.append(other)
    return found


def window_peers(dp, me, steps, z_lo_bits, tensor_half, z_all):
    low = 1 << len(z_lo_bits)
    unit = 1 << z_lo_bits[0]
    z_lo = lax.rem(lax.div(dp, unit), low)
    z_hi = lax.div(me, tensor_half)
    z = z_hi * low + z_lo
    found = []
    for step in steps:
        other = lax.rem(z + step + z_all, z_all)
        other_hi = lax.div(other, low)
        other_lo = other - other_hi * low
        found.append((dp + (other_lo - z_lo) * unit, me + (other_hi - z_hi) * tensor_half))
    return found


def segment_mask(seg_row):
    rows = seg_row.shape[1]
    seg = seg_row.astype(jnp.float32)
    seg_col = jnp.broadcast_to(seg, (128, rows)).T
    return [
        jnp.where(seg_col == seg[:, a * 128:(a + 1) * 128], 1.0, 0.0).astype(jnp.bfloat16) for a in range(rows // 128)
    ]


def row_coefs(tokens, gath, same, row_cap, count):
    nt = gath.shape[0]
    rows = row_cap.shape[1]
    half = rows // nt
    bf16, f32 = jnp.bfloat16, jnp.float32
    lane = lax.broadcasted_iota(jnp.int32, (nt, 128), 1)
    other = pltpu.roll(gath, half, 1)
    ratio = jnp.where(lane < half, gath, other)
    adv = jnp.where(lane < half, other, gath)
    place = lax.broadcasted_iota(jnp.int32, (nt, rows), 1) // half
    mine = place == lax.broadcasted_iota(jnp.int32, (nt, rows), 0)
    copies = rows // 128
    ratio = jnp.where(mine, jnp.concatenate([ratio] * copies, axis=1), 0.0)
    adv = jnp.sum(jnp.where(mine, jnp.concatenate([adv] * copies, axis=1), 0.0), axis=0, keepdims=True)
    hi = ratio.astype(bf16).astype(f32)
    mid = (ratio - hi).astype(bf16).astype(f32)
    low = ratio - hi - mid
    ones = jnp.ones((nt, rows), f32)
    left = jnp.concatenate([hi, mid, low, ones], axis=0).astype(bf16)
    sums = jnp.dot(left, same, preferred_element_type=f32)
    seg_sum = jnp.sum(sums[:3 * nt], axis=0, keepdims=True)
    seg_len = sums[3 * nt:3 * nt + 1]
    weight = jnp.minimum(jnp.exp(seg_sum / seg_len), row_cap)
    live = lax.broadcasted_iota(jnp.int32, (1, rows), 1) < count
    return jnp.where(live, -adv * weight * tokens, 0.0)


def block_kernel(tokens, plane_bits, z_lo_bits, z_all, nt, cnt_s,
                 new_hbm, old_hbm, adv_hbm, caps_hbm, seq_hbm, seg_hbm, ver_hbm, q_hbm, k_hbm, v_hbm, g_hbm,
                 dq_hbm, dk_ref, dv_ref, coef_ref,
                 q, k, v, g, dq, cq, cg, probs_t, dscore_t, k_t, bias, same, row_cap, dk_sum, dv_sum,
                 caps_s, seq_ref, seg_ref, ver_ref,
                 new_v, old_v, adv_v, own_row, rows_in, cnt_row, cnt_rows, part_row, part_rows,
                 sems, load_sem, send_sem, recv_sem):
    rows, columns = q.shape
    heads = columns // HEAD_DIM
    tiles = rows // TILE
    bf16, f32 = jnp.bfloat16, jnp.float32
    scale = HEAD_DIM ** -0.5
    factor = scale * math.log2(math.e)

    dp = lax.axis_index("dp")
    me = lax.axis_index("tensor")
    owners = partners(me, range(nt.bit_length() - 1))
    tensor_peers = [(dp, t) for t in owners]
    plane_peers = [(d, me) for d in partners(dp, plane_bits)]
    low = 1 << len(z_lo_bits)
    steps = [n for n in range(1 - low // 2, low // 2 + 1) if n != 0]
    from_window = window_peers(dp, me, steps, z_lo_bits, nt // 2, z_all)
    to_window = window_peers(dp, me, [-n for n in steps], z_lo_bits, nt // 2, z_all)
    planes = len(plane_peers) + 1

    barrier = pltpu.get_barrier_semaphore()
    for peer in tensor_peers + plane_peers + from_window:
        pl.semaphore_signal(barrier, inc=1, device_id=peer, device_id_type=MESH)

    def start_all(pairs, sem, first):
        copies = [pltpu.make_async_copy(src, dst, sem.at[first + n]) for n, (src, dst) in enumerate(pairs)]
        for copy in copies:
            copy.start()
        return copies

    def tile_rows(i):
        return pl.ds(i * TILE, TILE)

    own_in = start_all(((new_hbm, new_v), (old_hbm, old_v), (adv_hbm, adv_v)), load_sem, 0)
    small_in = start_all(((seq_hbm, seq_ref), (seg_hbm, seg_ref), (ver_hbm, ver_ref), (caps_hbm, caps_s),
                          (k_hbm, k), (v_hbm, v)), sems, 0)
    wide_in = [start_all(((q_hbm.at[tile_rows(i)], q.at[tile_rows(i)]), (g_hbm.at[tile_rows(i)], g.at[tile_rows(i)])),
                         sems, 6 + 2 * i) for i in range(tiles)]
    dq_out = [pltpu.make_async_copy(dq.at[tile_rows(i)], dq_hbm.at[tile_rows(i)], sems.at[6 + 2 * tiles + i])
              for i in range(tiles)]

    def send(src, dst, n, peer):
        pltpu.make_async_remote_copy(
            src_ref=src, dst_ref=dst, send_sem=send_sem.at[n], recv_sem=recv_sem.at[n],
            device_id=peer, device_id_type=MESH).start()

    def drain(buffer, n, sem):
        span = buffer.at[pl.ds(0, n)]
        pltpu.make_async_copy(span, span, sem).wait()

    def communicate():
        for load in own_in:
            load.wait()
        own_row[0] = jnp.concatenate([new_v[...] - old_v[...], adv_v[...]], axis=1)
        cnt_row[0] = jnp.full((1, 128), cnt_s[0].astype(f32), f32)
        pl.semaphore_wait(barrier, len(tensor_peers) + len(plane_peers) + len(to_window))
        for n, peer in enumerate(tensor_peers):
            send(own_row, rows_in.at[pl.ds(n, 1)], 1, peer)
        for n, peer in enumerate(plane_peers):
            send(cnt_row, cnt_rows.at[pl.ds(n, 1)], 0, peer)
        drain(cnt_rows, planes - 1, recv_sem.at[0])
        part = cnt_row[0]
        for n in range(planes - 1):
            part = part + cnt_rows[n]
        part_row[0] = part
        for n, peer in enumerate(to_window):
            send(part_row, part_rows.at[pl.ds(n, 1)], 2, peer)

    def head_pair(ref, i, p):
        return jnp.concatenate(
            [ref[i * TILE:(i + 1) * TILE, (2 * p + n) * HEAD_DIM:(2 * p + n + 1) * HEAD_DIM] for n in range(2)],
            axis=0)

    contract_last = (((1,), (1,)), ((), ()))
    far = me >= nt // 2

    @pl.when(far)
    def _():
        communicate()

    for load in small_in:
        load.wait()
    cap = jnp.zeros((1, rows), f32)
    for n in range(caps_s.shape[0]):
        cap = jnp.where(ver_ref[...] == n, caps_s[n], cap)
    row_cap[...] = cap
    for a, part in enumerate(segment_mask(seg_ref[...])):
        same[:, a * 128:(a + 1) * 128] = part
    k_t[...] = k[...].astype(f32).T.astype(bf16)
    for i in range(tiles):
        span = (i + 1) * TILE
        row_j = lax.broadcasted_iota(jnp.int32, (span, TILE), 0)
        col_t = lax.broadcasted_iota(jnp.int32, (span, TILE), 1) + i * TILE
        begin = seq_ref[:, i * TILE:(i + 1) * TILE]
        bias[0:span, :] = jnp.where((row_j >= begin) & (row_j <= col_t), 0.0, NEG)
        for load in wide_in[i]:
            load.wait()
        for p in range(heads // 2):
            scores = lax.dot_general(k[0:span, :], head_pair(q, i, p), contract_last, preferred_element_type=f32)
            d_prob = lax.dot_general(v[0:span, :], head_pair(g, i, p), contract_last, preferred_element_type=f32)
            scores = scores + jnp.concatenate([bias[0:span, :]] * 2, axis=1)
            top = jnp.max(scores, axis=0, keepdims=True)
            mass = jnp.exp2((scores - top) * factor)
            norm = 1.0 / jnp.sum(mass, axis=0, keepdims=True)
            delta = jnp.sum(mass * d_prob, axis=0, keepdims=True) * norm
            probs = mass * norm
            lanes = slice(i * columns + 2 * p * TILE, i * columns + 2 * (p + 1) * TILE)
            probs_t[0:span, lanes] = probs.astype(bf16)
            dscore_t[0:span, lanes] = (probs * (d_prob - delta)).astype(bf16)
        dq_t = jnp.dot(k_t[:, 0:span], dscore_t[0:span, i * columns:(i + 1) * columns],
                       preferred_element_type=f32) * scale
        for h in range(heads):
            dq[i * TILE:(i + 1) * TILE, h * HEAD_DIM:(h + 1) * HEAD_DIM] = (
                dq_t[:, h * TILE:(h + 1) * TILE].T.astype(bf16))
        dq_out[i].start()

    @pl.when(jnp.logical_not(far))
    def _():
        communicate()

    drain(rows_in, nt - 1, recv_sem.at[1])
    owner_row = lax.broadcasted_iota(jnp.int32, (nt, 128), 0)
    gathered = jnp.broadcast_to(own_row[0], (nt, 128))
    for n in range(nt - 1):
        gathered = jnp.where(owner_row == owners[n], jnp.broadcast_to(rows_in[n], (nt, 128)), gathered)
    coef = row_coefs(tokens, gathered, same[...], row_cap[...], cnt_s[0])
    coef_col = jnp.broadcast_to(coef, (HEAD_DIM, rows)).T
    for h in range(heads):
        lanes = slice(h * HEAD_DIM, (h + 1) * HEAD_DIM)
        cg[:, lanes] = (g[:, lanes].astype(f32) * coef_col).astype(bf16)
        cq[:, lanes] = (q[:, lanes].astype(f32) * coef_col).astype(bf16)
    for j in range(tiles):
        lanes = slice(j * columns, tiles * columns)
        stack = [(i, h) for i in range(j, tiles) for h in range(heads)]
        for source, right, target in ((probs_t, cg, dv_sum), (dscore_t, cq, dk_sum)):
            stacked = jnp.concatenate(
                [right[i * TILE:(i + 1) * TILE, h * HEAD_DIM:(h + 1) * HEAD_DIM] for i, h in stack], axis=0)
            target[j * TILE:(j + 1) * TILE, :] = jnp.dot(
                source[j * TILE:(j + 1) * TILE, lanes], stacked, preferred_element_type=f32)
    drain(part_rows, low - 1, recv_sem.at[2])
    total = part_row[0]
    for n in range(low - 1):
        total = total + part_rows[n]
    inverse = jnp.where(total > 0.0, 1.0 / total, 0.0)
    coef_ref[...] = coef * jnp.concatenate([inverse] * (rows // 128), axis=1)
    dv_ref[...] = (dv_sum[...] * inverse).astype(bf16)
    dk_ref[...] = (dk_sum[...] * (inverse * scale)).astype(bf16)
    drain(rows_in, nt - 1, send_sem.at[1])
    drain(cnt_rows, planes - 1, send_sem.at[0])
    drain(part_rows, low - 1, send_sem.at[2])
    for i in range(tiles):
        dq_out[i].wait()


def block(tokens, bits, nt, cnt, logp_new, logp_old, advantage, caps, seq_begin, seg_begin, version, q, k, v, g):
    plane_bits, z_lo_bits, z_all = bits
    rows, columns = q.shape
    own = logp_new.shape[0]
    tiles = rows // TILE
    planes, low = 1 << len(plane_bits), 1 << len(z_lo_bits)
    bf16, f32, i32 = jnp.bfloat16, jnp.float32, jnp.int32
    hbm = pl.BlockSpec(memory_space=pltpu.HBM)
    vmem = pl.BlockSpec(memory_space=pltpu.VMEM)
    wide, narrow = (rows, columns), (rows, HEAD_DIM)
    dma = pltpu.SemaphoreType.DMA
    return pl.pallas_call(
        functools.partial(block_kernel, tokens, plane_bits, z_lo_bits, z_all, nt),
        out_shape=(jax.ShapeDtypeStruct(wide, bf16), jax.ShapeDtypeStruct(narrow, bf16),
                   jax.ShapeDtypeStruct(narrow, bf16), jax.ShapeDtypeStruct((1, rows), f32)),
        in_specs=[pl.BlockSpec(memory_space=pltpu.SMEM)] + [hbm] * 11,
        out_specs=(hbm, vmem, vmem, vmem),
        scratch_shapes=[
            pltpu.VMEM(wide, bf16), pltpu.VMEM(narrow, bf16), pltpu.VMEM(narrow, bf16), pltpu.VMEM(wide, bf16),
            pltpu.VMEM(wide, bf16), pltpu.VMEM(wide, bf16), pltpu.VMEM(wide, bf16),
            pltpu.VMEM((rows, tiles * columns), bf16), pltpu.VMEM((rows, tiles * columns), bf16),
            pltpu.VMEM((HEAD_DIM, rows), bf16), pltpu.VMEM((rows, TILE), f32),
            pltpu.VMEM((rows, rows), bf16), pltpu.VMEM((1, rows), f32),
            pltpu.VMEM(narrow, f32), pltpu.VMEM(narrow, f32),
            pltpu.SMEM(caps.shape, f32),
            pltpu.VMEM((1, rows), i32), pltpu.VMEM((1, rows), i32), pltpu.VMEM((1, rows), i32),
            pltpu.VMEM((1, own), f32), pltpu.VMEM((1, own), f32), pltpu.VMEM((1, own), f32),
            pltpu.VMEM((1, 1, 128), f32), pltpu.VMEM((nt - 1, 1, 128), f32),
            pltpu.VMEM((1, 1, 128), f32), pltpu.VMEM((planes - 1, 1, 128), f32),
            pltpu.VMEM((1, 1, 128), f32), pltpu.VMEM((low - 1, 1, 128), f32),
            dma((6 + 3 * tiles,)), dma((3,)), dma((3,)), dma((3,)),
        ],
        compiler_params=pltpu.CompilerParams(
            collective_id=0, has_side_effects=True, vmem_limit_bytes=58 * 2**20),
        name="block",
    )(cnt, *in_hbm(logp_new.reshape(1, own), logp_old.reshape(1, own), advantage.reshape(1, own), caps,
                   seq_begin.reshape(1, rows), seg_begin.reshape(1, rows), version.reshape(1, rows), q, k, v, g))


def finish_kernel(coef_hbm, dq_in, dk_in, dv_in, dq_hbm, dk_hbm, dv_hbm, coef, dq, sems):
    rows, columns = dq.shape
    tiles = rows // TILE
    coef_load = pltpu.make_async_copy(coef_hbm, coef, sems.at[0])
    passed = [pltpu.make_async_copy(dk_in, dk_hbm, sems.at[1]), pltpu.make_async_copy(dv_in, dv_hbm, sems.at[2])]
    loads = [pltpu.make_async_copy(dq_in.at[pl.ds(i * TILE, TILE)], dq.at[pl.ds(i * TILE, TILE)], sems.at[3 + i])
             for i in range(tiles)]
    stores = [pltpu.make_async_copy(dq.at[pl.ds(i * TILE, TILE)], dq_hbm.at[pl.ds(i * TILE, TILE)],
                                    sems.at[3 + tiles + i]) for i in range(tiles)]
    for copy in [coef_load] + loads + passed:
        copy.start()
    coef_load.wait()
    coef_col = jnp.broadcast_to(coef[...], (HEAD_DIM, rows)).T
    for i in range(tiles):
        here = slice(i * TILE, (i + 1) * TILE)
        loads[i].wait()
        for h in range(columns // HEAD_DIM):
            lanes = slice(h * HEAD_DIM, (h + 1) * HEAD_DIM)
            dq[here, lanes] = (dq[here, lanes].astype(jnp.float32) * coef_col[here]).astype(dq.dtype)
        stores[i].start()
    for copy in stores + passed:
        copy.wait()


def finish(coef, dq, dk, dv):
    hbm = pl.BlockSpec(memory_space=pltpu.HBM)
    rows = dq.shape[0]
    return pl.pallas_call(
        finish_kernel,
        out_shape=tuple(jax.ShapeDtypeStruct(a.shape, a.dtype) for a in (dq, dk, dv)),
        in_specs=[hbm] * 4,
        out_specs=(hbm,) * 3,
        scratch_shapes=[pltpu.VMEM(coef.shape, jnp.float32), pltpu.VMEM(dq.shape, dq.dtype),
                        pltpu.SemaphoreType.DMA((3 + 2 * (rows // TILE),))],
        compiler_params=pltpu.CompilerParams(vmem_limit_bytes=58 * 2**20),
        name="finish",
    )(*in_hbm(coef, dq, dk, dv))


def solution(mesh):
    blocks, nt = mesh.shape["dp"], mesh.shape["tensor"]
    top = blocks.bit_length() - 1
    plane_bits, z_lo_bits = (0, top - 2, top - 1), tuple(range(1, top - 2))
    bits = (plane_bits, z_lo_bits, 2 << len(z_lo_bits))

    def local(query_heads, key_heads, value_heads, logp_grad, logp_new, logp_old, advantage, ratio_caps,
              live_counts, seq_begin, seg_begin, policy_version):
        tokens = float(query_heads.shape[0] * blocks)
        dq, dk, dv, coef = block(tokens, bits, nt, live_counts, logp_new, logp_old, advantage, ratio_caps,
                                 seq_begin, seg_begin, policy_version, query_heads, key_heads, value_heads, logp_grad)
        return finish(coef, dq, dk, dv)

    row, every = P("dp"), P(("dp", "tensor"))
    both = P("dp", "tensor")
    return jax.shard_map(
        local,
        mesh=mesh,
        in_specs=(both, both, both, both, every, every, every, P(), row, row, row, row),
        out_specs=(both, both, both),
        check_vma=False,
    )
```

```python
import functools
import math

import jax
import jax.numpy as jnp
from jax import lax
from jax.experimental import pallas as pl
from jax.experimental.pallas import tpu as pltpu
from jax.sharding import PartitionSpec as P

HEAD_DIM = 128
TILE = 128
MESH = pl.DeviceIdType.MESH
NEG = -1e30


def in_hbm(*arrays):
    return [pltpu.with_memory_space_constraint(a, pltpu.HBM) for a in arrays]


def flips(index, bits):
    return [(1 << b) * (1 - 2 * lax.rem(lax.div(index, 1 << b), 2)) for b in bits]


def partners(index, bits):
    deltas = flips(index, bits)
    found = []
    for mask in range(1, 1 << len(bits)):
        other = index
        for n, delta in enumerate(deltas):
            if mask >> n & 1:
                other = other + delta
        found.append(other)
    return found


def segment_mask(seg_row):
    rows = seg_row.shape[1]
    seg = seg_row.astype(jnp.float32)
    seg_col = jnp.broadcast_to(seg, (128, rows)).T
    return [
        jnp.where(seg_col == seg[:, a * 128:(a + 1) * 128], 1.0, 0.0).astype(jnp.bfloat16) for a in range(rows // 128)
    ]


def row_coefs(tokens, gath, same, row_cap, count):
    nt = gath.shape[0]
    rows = row_cap.shape[1]
    half = rows // nt
    bf16, f32 = jnp.bfloat16, jnp.float32
    lane = lax.broadcasted_iota(jnp.int32, (nt, 128), 1)
    other = pltpu.roll(gath, half, 1)
    ratio = jnp.where(lane < half, gath, other)
    adv = jnp.where(lane < half, other, gath)
    place = lax.broadcasted_iota(jnp.int32, (nt, rows), 1) // half
    mine = place == lax.broadcasted_iota(jnp.int32, (nt, rows), 0)
    copies = rows // 128
    ratio = jnp.where(mine, jnp.concatenate([ratio] * copies, axis=1), 0.0)
    adv = jnp.sum(jnp.where(mine, jnp.concatenate([adv] * copies, axis=1), 0.0), axis=0, keepdims=True)
    hi = ratio.astype(bf16).astype(f32)
    mid = (ratio - hi).astype(bf16).astype(f32)
    low = ratio - hi - mid
    ones = jnp.ones((nt, rows), f32)
    left = jnp.concatenate([hi, mid, low, ones], axis=0).astype(bf16)
    sums = jnp.dot(left, same, preferred_element_type=f32)
    seg_sum = jnp.sum(sums[:3 * nt], axis=0, keepdims=True)
    seg_len = sums[3 * nt:3 * nt + 1]
    weight = jnp.minimum(jnp.exp(seg_sum / seg_len), row_cap)
    live = lax.broadcasted_iota(jnp.int32, (1, rows), 1) < count
    return jnp.where(live, -adv * weight * tokens, 0.0)


def block_kernel(tokens, plane_bits, line_bits, nt, cnt_s,
                 new_hbm, old_hbm, adv_hbm, caps_hbm, seq_hbm, seg_hbm, ver_hbm, q_hbm, k_hbm, v_hbm, g_hbm,
                 dq, dk_ref, dv_ref, coef_ref,
                 q, k, v, g, cq, cg, probs_t, dscore_t, k_t, bias, same, row_cap, dk_sum, dv_sum,
                 caps_s, seq_ref, seg_ref, ver_ref,
                 new_v, old_v, adv_v, own_row, rows_in, cnt_row, cnt_rows, part_row, part_rows, total_row,
                 sems, load_sem, send_sem, recv_sem):
    rows, columns = q.shape
    heads = columns // HEAD_DIM
    tiles = rows // TILE
    bf16, f32 = jnp.bfloat16, jnp.float32
    scale = HEAD_DIM ** -0.5
    factor = scale * math.log2(math.e)

    dp = lax.axis_index("dp")
    me = lax.axis_index("tensor")
    owners = partners(me, range(nt.bit_length() - 1))
    tensor_peers = [(dp, t) for t in owners]
    plane_peers = [(d, me) for d in partners(dp, plane_bits)]
    half = nt // 2
    far = me >= half
    near = me < half
    line = [dp] + partners(dp, line_bits)
    far_line = [(d, me + half) for d in line]
    near_line = [(d, me - half) for d in line]

    barrier = pltpu.get_barrier_semaphore()

    def greet(peers):
        for peer in peers:
            pl.semaphore_signal(barrier, inc=1, device_id=peer, device_id_type=MESH)

    greet(tensor_peers)

    @pl.when(far)
    def _():
        greet(plane_peers)

    @pl.when(near)
    def _():
        greet(far_line[1:])

    def start_all(pairs, sem, first):
        copies = [pltpu.make_async_copy(src, dst, sem.at[first + n]) for n, (src, dst) in enumerate(pairs)]
        for copy in copies:
            copy.start()
        return copies

    def tile_rows(i):
        return pl.ds(i * TILE, TILE)

    own_in = start_all(((new_hbm, new_v), (old_hbm, old_v), (adv_hbm, adv_v)), load_sem, 0)
    small_in = start_all(((seq_hbm, seq_ref), (seg_hbm, seg_ref), (ver_hbm, ver_ref), (caps_hbm, caps_s),
                          (k_hbm, k), (v_hbm, v)), sems, 0)
    wide_in = [start_all(((q_hbm.at[tile_rows(i)], q.at[tile_rows(i)]), (g_hbm.at[tile_rows(i)], g.at[tile_rows(i)])),
                         sems, 6 + 2 * i) for i in range(tiles)]
    def send(src, dst, n, peer):
        pltpu.make_async_remote_copy(
            src_ref=src, dst_ref=dst, send_sem=send_sem.at[n], recv_sem=recv_sem.at[n],
            device_id=peer, device_id_type=MESH).start()

    def drain(buffer, n, sem):
        span = buffer.at[pl.ds(0, n)]
        pltpu.make_async_copy(span, span, sem).wait()

    def send_rows(signals):
        for load in own_in:
            load.wait()
        own_row[0] = jnp.concatenate([new_v[...] - old_v[...], adv_v[...]], axis=1)
        pl.semaphore_wait(barrier, signals)
        for n, peer in enumerate(tensor_peers):
            send(own_row, rows_in.at[pl.ds(n, 1)], 0, peer)

    def send_partial():
        for n, peer in enumerate(plane_peers):
            send(cnt_row, cnt_rows.at[pl.ds(n, 1)], 1, peer)
        drain(cnt_rows, len(plane_peers), recv_sem.at[1])
        part = cnt_row[0]
        for n in range(len(plane_peers)):
            part = part + cnt_rows[n]
        part_row[0] = part
        for n, peer in enumerate(near_line):
            send(part_row, part_rows.at[pl.ds(n, 1)], 2, peer)

    def send_total():
        drain(part_rows, len(line), recv_sem.at[2])
        total = part_rows[0]
        for n in range(1, len(line)):
            total = total + part_rows[n]
        total_row[0] = total
        send(total_row, total_row, 3, far_line[0])

    def head_pair(ref, i, p):
        return jnp.concatenate(
            [ref[i * TILE:(i + 1) * TILE, (2 * p + n) * HEAD_DIM:(2 * p + n + 1) * HEAD_DIM] for n in range(2)],
            axis=0)

    contract_last = (((1,), (1,)), ((), ()))

    @pl.when(far)
    def _():
        cnt_row[0] = jnp.full((1, 128), cnt_s[0].astype(f32), f32)
        send_rows(len(tensor_peers) + len(plane_peers) + len(line) - 1)
        send_partial()

    for load in small_in:
        load.wait()
    cap = jnp.zeros((1, rows), f32)
    for n in range(caps_s.shape[0]):
        cap = jnp.where(ver_ref[...] == n, caps_s[n], cap)
    row_cap[...] = cap
    for a, part in enumerate(segment_mask(seg_ref[...])):
        same[:, a * 128:(a + 1) * 128] = part
    k_t[...] = k[...].astype(f32).T.astype(bf16)
    for i in range(tiles):
        span = (i + 1) * TILE
        row_j = lax.broadcasted_iota(jnp.int32, (span, TILE), 0)
        col_t = lax.broadcasted_iota(jnp.int32, (span, TILE), 1) + i * TILE
        begin = seq_ref[:, i * TILE:(i + 1) * TILE]
        bias[0:span, :] = jnp.where((row_j >= begin) & (row_j <= col_t), 0.0, NEG)
        for load in wide_in[i]:
            load.wait()
        for p in range(heads // 2):
            scores = lax.dot_general(k[0:span, :], head_pair(q, i, p), contract_last, preferred_element_type=f32)
            d_prob = lax.dot_general(v[0:span, :], head_pair(g, i, p), contract_last, preferred_element_type=f32)
            scores = scores + jnp.concatenate([bias[0:span, :]] * 2, axis=1)
            top = jnp.max(scores, axis=0, keepdims=True)
            mass = jnp.exp2((scores - top) * factor)
            norm = 1.0 / jnp.sum(mass, axis=0, keepdims=True)
            delta = jnp.sum(mass * d_prob, axis=0, keepdims=True) * norm
            probs = mass * norm
            lanes = slice(i * columns + 2 * p * TILE, i * columns + 2 * (p + 1) * TILE)
            probs_t[0:span, lanes] = probs.astype(bf16)
            dscore_t[0:span, lanes] = (probs * (d_prob - delta)).astype(bf16)
        dq_t = jnp.dot(k_t[:, 0:span], dscore_t[0:span, i * columns:(i + 1) * columns],
                       preferred_element_type=f32) * scale
        for h in range(heads):
            dq[i * TILE:(i + 1) * TILE, h * HEAD_DIM:(h + 1) * HEAD_DIM] = (
                dq_t[:, h * TILE:(h + 1) * TILE].T.astype(bf16))

    @pl.when(near)
    def _():
        send_rows(len(tensor_peers))

    drain(rows_in, nt - 1, recv_sem.at[0])
    owner_row = lax.broadcasted_iota(jnp.int32, (nt, 128), 0)
    gathered = jnp.broadcast_to(own_row[0], (nt, 128))
    for n in range(nt - 1):
        gathered = jnp.where(owner_row == owners[n], jnp.broadcast_to(rows_in[n], (nt, 128)), gathered)
    coef = row_coefs(tokens, gathered, same[...], row_cap[...], cnt_s[0])

    @pl.when(near)
    def _():
        send_total()

    coef_col = jnp.broadcast_to(coef, (HEAD_DIM, rows)).T
    for h in range(heads):
        lanes = slice(h * HEAD_DIM, (h + 1) * HEAD_DIM)
        cg[:, lanes] = (g[:, lanes].astype(f32) * coef_col).astype(bf16)
        cq[:, lanes] = (q[:, lanes].astype(f32) * coef_col).astype(bf16)
    for j in range(tiles):
        lanes = slice(j * columns, tiles * columns)
        stack = [(i, h) for i in range(j, tiles) for h in range(heads)]
        for source, right, target in ((probs_t, cg, dv_sum), (dscore_t, cq, dk_sum)):
            stacked = jnp.concatenate(
                [right[i * TILE:(i + 1) * TILE, h * HEAD_DIM:(h + 1) * HEAD_DIM] for i, h in stack], axis=0)
            target[j * TILE:(j + 1) * TILE, :] = jnp.dot(
                source[j * TILE:(j + 1) * TILE, lanes], stacked, preferred_element_type=f32)

    @pl.when(far)
    def _():
        drain(total_row, 1, recv_sem.at[3])

    total = total_row[0]
    inverse = jnp.where(total > 0.0, 1.0 / total, 0.0)
    coef_ref[...] = coef * jnp.concatenate([inverse] * (rows // 128), axis=1)
    dv_ref[...] = (dv_sum[...] * inverse).astype(bf16)
    dk_ref[...] = (dk_sum[...] * (inverse * scale)).astype(bf16)
    drain(rows_in, nt - 1, send_sem.at[0])

    @pl.when(far)
    def _():
        drain(cnt_rows, len(plane_peers), send_sem.at[1])
        drain(part_rows, len(line), send_sem.at[2])

    @pl.when(near)
    def _():
        drain(total_row, 1, send_sem.at[3])


def block(tokens, bits, nt, cnt, logp_new, logp_old, advantage, caps, seq_begin, seg_begin, version, q, k, v, g):
    plane_bits, line_bits = bits
    rows, columns = q.shape
    own = logp_new.shape[0]
    tiles = rows // TILE
    planes, low = 1 << len(plane_bits), 1 << len(line_bits)
    bf16, f32, i32 = jnp.bfloat16, jnp.float32, jnp.int32
    hbm = pl.BlockSpec(memory_space=pltpu.HBM)
    vmem = pl.BlockSpec(memory_space=pltpu.VMEM)
    wide, narrow = (rows, columns), (rows, HEAD_DIM)
    dma = pltpu.SemaphoreType.DMA
    return pl.pallas_call(
        functools.partial(block_kernel, tokens, plane_bits, line_bits, nt),
        out_shape=(jax.ShapeDtypeStruct(wide, bf16), jax.ShapeDtypeStruct(narrow, bf16),
                   jax.ShapeDtypeStruct(narrow, bf16), jax.ShapeDtypeStruct((1, rows), f32)),
        in_specs=[pl.BlockSpec(memory_space=pltpu.SMEM)] + [hbm] * 11,
        out_specs=(vmem,) * 4,
        scratch_shapes=[
            pltpu.VMEM(wide, bf16), pltpu.VMEM(narrow, bf16), pltpu.VMEM(narrow, bf16), pltpu.VMEM(wide, bf16),
            pltpu.VMEM(wide, bf16), pltpu.VMEM(wide, bf16),
            pltpu.VMEM((rows, tiles * columns), bf16), pltpu.VMEM((rows, tiles * columns), bf16),
            pltpu.VMEM((HEAD_DIM, rows), bf16), pltpu.VMEM((rows, TILE), f32),
            pltpu.VMEM((rows, rows), bf16), pltpu.VMEM((1, rows), f32),
            pltpu.VMEM(narrow, f32), pltpu.VMEM(narrow, f32),
            pltpu.SMEM(caps.shape, f32),
            pltpu.VMEM((1, rows), i32), pltpu.VMEM((1, rows), i32), pltpu.VMEM((1, rows), i32),
            pltpu.VMEM((1, own), f32), pltpu.VMEM((1, own), f32), pltpu.VMEM((1, own), f32),
            pltpu.VMEM((1, 1, 128), f32), pltpu.VMEM((nt - 1, 1, 128), f32),
            pltpu.VMEM((1, 1, 128), f32), pltpu.VMEM((planes - 1, 1, 128), f32),
            pltpu.VMEM((1, 1, 128), f32), pltpu.VMEM((low, 1, 128), f32), pltpu.VMEM((1, 1, 128), f32),
            dma((6 + 2 * tiles,)), dma((3,)), dma((4,)), dma((4,)),
        ],
        compiler_params=pltpu.CompilerParams(
            collective_id=0, has_side_effects=True, vmem_limit_bytes=32 * 2**20),
        name="block",
    )(cnt, *in_hbm(logp_new.reshape(1, own), logp_old.reshape(1, own), advantage.reshape(1, own), caps,
                   seq_begin.reshape(1, rows), seg_begin.reshape(1, rows), version.reshape(1, rows), q, k, v, g))


def finish_kernel(coef, dq_in, dk_in, dv_in, dq_hbm, dk_hbm, dv_hbm, dq, sems):
    rows, columns = dq.shape
    tiles = rows // TILE
    passed = [pltpu.make_async_copy(dk_in, dk_hbm, sems.at[0]), pltpu.make_async_copy(dv_in, dv_hbm, sems.at[1])]
    stores = [pltpu.make_async_copy(dq.at[pl.ds(i * TILE, TILE)], dq_hbm.at[pl.ds(i * TILE, TILE)], sems.at[2 + i])
              for i in range(tiles)]
    for copy in passed:
        copy.start()
    for i in range(tiles):
        here = slice(i * TILE, (i + 1) * TILE)
        coef_col = jnp.broadcast_to(coef[:, here], (HEAD_DIM, TILE)).T
        for h in range(columns // HEAD_DIM):
            lanes = slice(h * HEAD_DIM, (h + 1) * HEAD_DIM)
            dq[here, lanes] = (dq_in[here, lanes].astype(jnp.float32) * coef_col).astype(dq.dtype)
        stores[i].start()
    for copy in stores + passed:
        copy.wait()


def finish(coef, dq, dk, dv):
    hbm = pl.BlockSpec(memory_space=pltpu.HBM)
    vmem = pl.BlockSpec(memory_space=pltpu.VMEM)
    return pl.pallas_call(
        finish_kernel,
        out_shape=tuple(jax.ShapeDtypeStruct(a.shape, a.dtype) for a in (dq, dk, dv)),
        in_specs=[vmem] * 4,
        out_specs=(hbm,) * 3,
        scratch_shapes=[pltpu.VMEM(dq.shape, dq.dtype), pltpu.SemaphoreType.DMA((2 + dq.shape[0] // TILE,))],
        compiler_params=pltpu.CompilerParams(vmem_limit_bytes=32 * 2**20),
        name="finish",
    )(coef, dq, dk, dv)


def solution(mesh):
    blocks, nt = mesh.shape["dp"], mesh.shape["tensor"]
    top = blocks.bit_length() - 1
    bits = ((0, top - 2, top - 1), tuple(range(1, top - 2)))

    def local(query_heads, key_heads, value_heads, logp_grad, logp_new, logp_old, advantage, ratio_caps,
              live_counts, seq_begin, seg_begin, policy_version):
        tokens = float(query_heads.shape[0] * blocks)
        dq, dk, dv, coef = block(tokens, bits, nt, live_counts, logp_new, logp_old, advantage, ratio_caps,
                                 seq_begin, seg_begin, policy_version, query_heads, key_heads, value_heads, logp_grad)
        return finish(coef, dq, dk, dv)

    row, every = P("dp"), P(("dp", "tensor"))
    both = P("dp", "tensor")
    return jax.shard_map(
        local,
        mesh=mesh,
        in_specs=(both, both, both, both, every, every, every, P(), row, row, row, row),
        out_specs=(both, both, both),
        check_vma=False,
    )
```

```python
import functools
import math

import jax
import jax.numpy as jnp
from jax import lax
from jax.experimental import pallas as pl
from jax.experimental.pallas import tpu as pltpu
from jax.sharding import PartitionSpec as P

HEAD_DIM = 128
TILE = 128
MESH = pl.DeviceIdType.MESH
NEG = -1e30


def in_hbm(*arrays):
    return [pltpu.with_memory_space_constraint(a, pltpu.HBM) for a in arrays]


def flips(index, bits):
    return [(1 << b) * (1 - 2 * lax.rem(lax.div(index, 1 << b), 2)) for b in bits]


def partners(index, bits):
    deltas = flips(index, bits)
    found = []
    for mask in range((1 << len(bits)) - 1, 0, -1):
        other = index
        for n, delta in enumerate(deltas):
            if mask >> n & 1:
                other = other + delta
        found.append(other)
    return found


def segment_mask(seg_row):
    rows = seg_row.shape[1]
    seg = seg_row.astype(jnp.float32)
    seg_col = jnp.broadcast_to(seg, (128, rows)).T
    return [
        jnp.where(seg_col == seg[:, a * 128:(a + 1) * 128], 1.0, 0.0).astype(jnp.bfloat16) for a in range(rows // 128)
    ]


def row_coefs(tokens, gath, same, row_cap, count):
    nt = gath.shape[0]
    rows = row_cap.shape[1]
    half = rows // nt
    bf16, f32 = jnp.bfloat16, jnp.float32
    lane = lax.broadcasted_iota(jnp.int32, (nt, 128), 1)
    other = pltpu.roll(gath, half, 1)
    ratio = jnp.where(lane < half, gath, other)
    adv = jnp.where(lane < half, other, gath)
    place = lax.broadcasted_iota(jnp.int32, (nt, rows), 1) // half
    mine = place == lax.broadcasted_iota(jnp.int32, (nt, rows), 0)
    copies = rows // 128
    ratio = jnp.where(mine, jnp.concatenate([ratio] * copies, axis=1), 0.0)
    adv = jnp.sum(jnp.where(mine, jnp.concatenate([adv] * copies, axis=1), 0.0), axis=0, keepdims=True)
    hi = ratio.astype(bf16).astype(f32)
    mid = (ratio - hi).astype(bf16).astype(f32)
    low = ratio - hi - mid
    ones = jnp.ones((nt, rows), f32)
    left = jnp.concatenate([hi, mid, low, ones], axis=0).astype(bf16)
    sums = jnp.dot(left, same, preferred_element_type=f32)
    seg_sum = jnp.sum(sums[:3 * nt], axis=0, keepdims=True)
    seg_len = sums[3 * nt:3 * nt + 1]
    weight = jnp.minimum(jnp.exp(seg_sum / seg_len), row_cap)
    live = lax.broadcasted_iota(jnp.int32, (1, rows), 1) < count
    return jnp.where(live, -adv * weight * tokens, 0.0)


def block_kernel(tokens, plane_bits, line_bits, nt, cnt_s,
                 new_hbm, old_hbm, adv_hbm, caps_hbm, seq_hbm, seg_hbm, ver_hbm, q_hbm, k_hbm, v_hbm, g_hbm,
                 dq, dk_ref, dv_ref, coef_ref,
                 q, k, v, g, cq, cg, probs_t, dscore_t, k_t, bias, same, row_cap, dk_sum, dv_sum,
                 caps_s, seq_ref, seg_ref, ver_ref,
                 new_v, old_v, adv_v, own_row, rows_in, cnt_row, cnt_rows, part_row, part_rows,
                 sems, load_sem, send_sem, recv_sem):
    rows, columns = q.shape
    heads = columns // HEAD_DIM
    tiles = rows // TILE
    bf16, f32 = jnp.bfloat16, jnp.float32
    scale = HEAD_DIM ** -0.5
    factor = scale * math.log2(math.e)

    dp = lax.axis_index("dp")
    me = lax.axis_index("tensor")
    owners = partners(me, range(nt.bit_length() - 1))
    tensor_peers = [(dp, t) for t in owners]
    plane_peers = [(d, me) for d in partners(dp, plane_bits)]
    half = nt // 2
    far = me >= half
    across = lax.rem(me + half, nt)
    line_peers = [(d, across) for d in partners(dp, line_bits)]
    cross, beside = tensor_peers[:half], tensor_peers[half:]
    greeted = len(tensor_peers) + len(plane_peers) + len(line_peers)

    barrier = pltpu.get_barrier_semaphore()
    for peer in beside + plane_peers + cross + line_peers:
        pl.semaphore_signal(barrier, inc=1, device_id=peer, device_id_type=MESH)

    def start_all(pairs, sem, first):
        copies = [pltpu.make_async_copy(src, dst, sem.at[first + n]) for n, (src, dst) in enumerate(pairs)]
        for copy in copies:
            copy.start()
        return copies

    def tile_rows(i):
        return pl.ds(i * TILE, TILE)

    own_in = start_all(((new_hbm, new_v), (old_hbm, old_v), (adv_hbm, adv_v)), load_sem, 0)
    small_in = start_all(((seq_hbm, seq_ref), (seg_hbm, seg_ref), (ver_hbm, ver_ref), (caps_hbm, caps_s),
                          (k_hbm, k), (v_hbm, v)), sems, 0)
    wide_in = [start_all(((q_hbm.at[tile_rows(i)], q.at[tile_rows(i)]), (g_hbm.at[tile_rows(i)], g.at[tile_rows(i)])),
                         sems, 6 + 2 * i) for i in range(tiles)]
    def send(src, dst, n, peer):
        pltpu.make_async_remote_copy(
            src_ref=src, dst_ref=dst, send_sem=send_sem.at[n], recv_sem=recv_sem.at[n],
            device_id=peer, device_id_type=MESH).start()

    def drain(buffer, n, sem):
        span = buffer.at[pl.ds(0, n)]
        pltpu.make_async_copy(span, span, sem).wait()

    def send_own():
        for load in own_in:
            load.wait()
        own_row[0] = jnp.concatenate([new_v[...] - old_v[...], adv_v[...]], axis=1)
        cnt_row[0] = jnp.full((1, 128), cnt_s[0].astype(f32), f32)
        pl.semaphore_wait(barrier, greeted)
        for n, peer in enumerate(tensor_peers):
            send(own_row, rows_in.at[pl.ds(n, 1)], 0, peer)
        for n, peer in enumerate(plane_peers):
            send(cnt_row, cnt_rows.at[pl.ds(n, 1)], 1, peer)

    def send_partial():
        drain(cnt_rows, len(plane_peers), recv_sem.at[1])
        part = cnt_row[0]
        for n in range(len(plane_peers)):
            part = part + cnt_rows[n]
        part_row[0] = part
        for n, peer in enumerate(line_peers + [(dp, across)]):
            send(part_row, part_rows.at[pl.ds(n, 1)], 2, peer)

    def head_pair(ref, i, p):
        return jnp.concatenate(
            [ref[i * TILE:(i + 1) * TILE, (2 * p + n) * HEAD_DIM:(2 * p + n + 1) * HEAD_DIM] for n in range(2)],
            axis=0)

    contract_last = (((1,), (1,)), ((), ()))

    @pl.when(far)
    def _():
        send_own()
        send_partial()

    for load in small_in:
        load.wait()
    cap = jnp.zeros((1, rows), f32)
    for n in range(caps_s.shape[0]):
        cap = jnp.where(ver_ref[...] == n, caps_s[n], cap)
    row_cap[...] = cap
    for a, part in enumerate(segment_mask(seg_ref[...])):
        same[:, a * 128:(a + 1) * 128] = part
    k_t[...] = k[...].astype(f32).T.astype(bf16)
    for i in range(tiles):
        span = (i + 1) * TILE
        row_j = lax.broadcasted_iota(jnp.int32, (span, TILE), 0)
        col_t = lax.broadcasted_iota(jnp.int32, (span, TILE), 1) + i * TILE
        begin = seq_ref[:, i * TILE:(i + 1) * TILE]
        bias[0:span, :] = jnp.where((row_j >= begin) & (row_j <= col_t), 0.0, NEG)
        for load in wide_in[i]:
            load.wait()
        for p in range(heads // 2):
            scores = lax.dot_general(k[0:span, :], head_pair(q, i, p), contract_last, preferred_element_type=f32)
            d_prob = lax.dot_general(v[0:span, :], head_pair(g, i, p), contract_last, preferred_element_type=f32)
            scores = scores + jnp.concatenate([bias[0:span, :]] * 2, axis=1)
            top = jnp.max(scores, axis=0, keepdims=True)
            mass = jnp.exp2((scores - top) * factor)
            norm = 1.0 / jnp.sum(mass, axis=0, keepdims=True)
            delta = jnp.sum(mass * d_prob, axis=0, keepdims=True) * norm
            probs = mass * norm
            lanes = slice(i * columns + 2 * p * TILE, i * columns + 2 * (p + 1) * TILE)
            probs_t[0:span, lanes] = probs.astype(bf16)
            dscore_t[0:span, lanes] = (probs * (d_prob - delta)).astype(bf16)
        dq_t = jnp.dot(k_t[:, 0:span], dscore_t[0:span, i * columns:(i + 1) * columns],
                       preferred_element_type=f32) * scale
        for h in range(heads):
            dq[i * TILE:(i + 1) * TILE, h * HEAD_DIM:(h + 1) * HEAD_DIM] = (
                dq_t[:, h * TILE:(h + 1) * TILE].T.astype(bf16))

    @pl.when(jnp.logical_not(far))
    def _():
        send_own()

    drain(rows_in, nt - 1, recv_sem.at[0])
    owner_row = lax.broadcasted_iota(jnp.int32, (nt, 128), 0)
    gathered = jnp.broadcast_to(own_row[0], (nt, 128))
    for n in range(nt - 1):
        gathered = jnp.where(owner_row == owners[n], jnp.broadcast_to(rows_in[n], (nt, 128)), gathered)
    coef = row_coefs(tokens, gathered, same[...], row_cap[...], cnt_s[0])

    @pl.when(jnp.logical_not(far))
    def _():
        send_partial()

    coef_col = jnp.broadcast_to(coef, (HEAD_DIM, rows)).T
    for h in range(heads):
        lanes = slice(h * HEAD_DIM, (h + 1) * HEAD_DIM)
        cg[:, lanes] = (g[:, lanes].astype(f32) * coef_col).astype(bf16)
        cq[:, lanes] = (q[:, lanes].astype(f32) * coef_col).astype(bf16)
    for j in range(tiles):
        lanes = slice(j * columns, tiles * columns)
        stack = [(i, h) for i in range(j, tiles) for h in range(heads)]
        for source, right, target in ((probs_t, cg, dv_sum), (dscore_t, cq, dk_sum)):
            stacked = jnp.concatenate(
                [right[i * TILE:(i + 1) * TILE, h * HEAD_DIM:(h + 1) * HEAD_DIM] for i, h in stack], axis=0)
            target[j * TILE:(j + 1) * TILE, :] = jnp.dot(
                source[j * TILE:(j + 1) * TILE, lanes], stacked, preferred_element_type=f32)
    drain(part_rows, len(line_peers) + 1, recv_sem.at[2])
    total = part_rows[0]
    for n in range(len(line_peers)):
        total = total + part_rows[n + 1]
    inverse = jnp.where(total > 0.0, 1.0 / total, 0.0)
    coef_ref[...] = coef * jnp.concatenate([inverse] * (rows // 128), axis=1)
    dv_ref[...] = (dv_sum[...] * inverse).astype(bf16)
    dk_ref[...] = (dk_sum[...] * (inverse * scale)).astype(bf16)
    drain(rows_in, nt - 1, send_sem.at[0])
    drain(cnt_rows, len(plane_peers), send_sem.at[1])
    drain(part_rows, len(line_peers) + 1, send_sem.at[2])


def block(tokens, bits, nt, cnt, logp_new, logp_old, advantage, caps, seq_begin, seg_begin, version, q, k, v, g):
    plane_bits, line_bits = bits
    rows, columns = q.shape
    own = logp_new.shape[0]
    tiles = rows // TILE
    planes, low = 1 << len(plane_bits), 1 << len(line_bits)
    bf16, f32, i32 = jnp.bfloat16, jnp.float32, jnp.int32
    hbm = pl.BlockSpec(memory_space=pltpu.HBM)
    vmem = pl.BlockSpec(memory_space=pltpu.VMEM)
    wide, narrow = (rows, columns), (rows, HEAD_DIM)
    dma = pltpu.SemaphoreType.DMA
    return pl.pallas_call(
        functools.partial(block_kernel, tokens, plane_bits, line_bits, nt),
        out_shape=(jax.ShapeDtypeStruct(wide, bf16), jax.ShapeDtypeStruct(narrow, bf16),
                   jax.ShapeDtypeStruct(narrow, bf16), jax.ShapeDtypeStruct((1, rows), f32)),
        in_specs=[pl.BlockSpec(memory_space=pltpu.SMEM)] + [hbm] * 11,
        out_specs=(vmem,) * 4,
        scratch_shapes=[
            pltpu.VMEM(wide, bf16), pltpu.VMEM(narrow, bf16), pltpu.VMEM(narrow, bf16), pltpu.VMEM(wide, bf16),
            pltpu.VMEM(wide, bf16), pltpu.VMEM(wide, bf16),
            pltpu.VMEM((rows, tiles * columns), bf16), pltpu.VMEM((rows, tiles * columns), bf16),
            pltpu.VMEM((HEAD_DIM, rows), bf16), pltpu.VMEM((rows, TILE), f32),
            pltpu.VMEM((rows, rows), bf16), pltpu.VMEM((1, rows), f32),
            pltpu.VMEM(narrow, f32), pltpu.VMEM(narrow, f32),
            pltpu.SMEM(caps.shape, f32),
            pltpu.VMEM((1, rows), i32), pltpu.VMEM((1, rows), i32), pltpu.VMEM((1, rows), i32),
            pltpu.VMEM((1, own), f32), pltpu.VMEM((1, own), f32), pltpu.VMEM((1, own), f32),
            pltpu.VMEM((1, 1, 128), f32), pltpu.VMEM((nt - 1, 1, 128), f32),
            pltpu.VMEM((1, 1, 128), f32), pltpu.VMEM((planes - 1, 1, 128), f32),
            pltpu.VMEM((1, 1, 128), f32), pltpu.VMEM((low, 1, 128), f32),
            dma((6 + 2 * tiles,)), dma((3,)), dma((3,)), dma((3,)),
        ],
        compiler_params=pltpu.CompilerParams(
            collective_id=0, has_side_effects=True, vmem_limit_bytes=32 * 2**20),
        name="block",
    )(cnt, *in_hbm(logp_new.reshape(1, own), logp_old.reshape(1, own), advantage.reshape(1, own), caps,
                   seq_begin.reshape(1, rows), seg_begin.reshape(1, rows), version.reshape(1, rows), q, k, v, g))


def finish_kernel(coef, dq_in, dk_in, dv_in, dq_hbm, dk_hbm, dv_hbm, dq, sems):
    rows, columns = dq.shape
    tiles = rows // TILE
    passed = [pltpu.make_async_copy(dk_in, dk_hbm, sems.at[0]), pltpu.make_async_copy(dv_in, dv_hbm, sems.at[1])]
    stores = [pltpu.make_async_copy(dq.at[pl.ds(i * TILE, TILE)], dq_hbm.at[pl.ds(i * TILE, TILE)], sems.at[2 + i])
              for i in range(tiles)]
    for copy in passed:
        copy.start()
    for i in range(tiles):
        here = slice(i * TILE, (i + 1) * TILE)
        coef_col = jnp.broadcast_to(coef[:, here], (HEAD_DIM, TILE)).T
        for h in range(columns // HEAD_DIM):
            lanes = slice(h * HEAD_DIM, (h + 1) * HEAD_DIM)
            dq[here, lanes] = (dq_in[here, lanes].astype(jnp.float32) * coef_col).astype(dq.dtype)
        stores[i].start()
    for copy in stores + passed:
        copy.wait()


def finish(coef, dq, dk, dv):
    hbm = pl.BlockSpec(memory_space=pltpu.HBM)
    vmem = pl.BlockSpec(memory_space=pltpu.VMEM)
    return pl.pallas_call(
        finish_kernel,
        out_shape=tuple(jax.ShapeDtypeStruct(a.shape, a.dtype) for a in (dq, dk, dv)),
        in_specs=[vmem] * 4,
        out_specs=(hbm,) * 3,
        scratch_shapes=[pltpu.VMEM(dq.shape, dq.dtype), pltpu.SemaphoreType.DMA((2 + dq.shape[0] // TILE,))],
        compiler_params=pltpu.CompilerParams(vmem_limit_bytes=32 * 2**20),
        name="finish",
    )(coef, dq, dk, dv)


def solution(mesh):
    blocks, nt = mesh.shape["dp"], mesh.shape["tensor"]
    top = blocks.bit_length() - 1
    bits = ((0, top - 2, top - 1), tuple(range(1, top - 2)))

    def local(query_heads, key_heads, value_heads, logp_grad, logp_new, logp_old, advantage, ratio_caps,
              live_counts, seq_begin, seg_begin, policy_version):
        tokens = float(query_heads.shape[0] * blocks)
        dq, dk, dv, coef = block(tokens, bits, nt, live_counts, logp_new, logp_old, advantage, ratio_caps,
                                 seq_begin, seg_begin, policy_version, query_heads, key_heads, value_heads, logp_grad)
        return finish(coef, dq, dk, dv)

    row, every = P("dp"), P(("dp", "tensor"))
    both = P("dp", "tensor")
    return jax.shard_map(
        local,
        mesh=mesh,
        in_specs=(both, both, both, both, every, every, every, P(), row, row, row, row),
        out_specs=(both, both, both),
        check_vma=False,
    )
```

```python
import functools
import math

import jax
import jax.numpy as jnp
from jax import lax
from jax.experimental import pallas as pl
from jax.experimental.pallas import tpu as pltpu
from jax.sharding import PartitionSpec as P

HEAD_DIM = 128
TILE = 128
MESH = pl.DeviceIdType.MESH
NEG = -1e30


def in_hbm(*arrays):
    return [pltpu.with_memory_space_constraint(a, pltpu.HBM) for a in arrays]


def flips(index, bits):
    return [(1 << b) * (1 - 2 * lax.rem(lax.div(index, 1 << b), 2)) for b in bits]


def partners(index, bits):
    deltas = flips(index, bits)
    found = []
    for mask in range((1 << len(bits)) - 1, 0, -1):
        other = index
        for n, delta in enumerate(deltas):
            if mask >> n & 1:
                other = other + delta
        found.append(other)
    return found


def segment_mask(seg_row):
    rows = seg_row.shape[1]
    seg = seg_row.astype(jnp.float32)
    seg_col = jnp.broadcast_to(seg, (128, rows)).T
    return [
        jnp.where(seg_col == seg[:, a * 128:(a + 1) * 128], 1.0, 0.0).astype(jnp.bfloat16) for a in range(rows // 128)
    ]


def row_coefs(tokens, gath, same, row_cap, count):
    nt = gath.shape[0]
    rows = row_cap.shape[1]
    half = rows // nt
    bf16, f32 = jnp.bfloat16, jnp.float32
    lane = lax.broadcasted_iota(jnp.int32, (nt, 128), 1)
    other = pltpu.roll(gath, half, 1)
    ratio = jnp.where(lane < half, gath, other)
    adv = jnp.where(lane < half, other, gath)
    place = lax.broadcasted_iota(jnp.int32, (nt, rows), 1) // half
    mine = place == lax.broadcasted_iota(jnp.int32, (nt, rows), 0)
    copies = rows // 128
    ratio = jnp.where(mine, jnp.concatenate([ratio] * copies, axis=1), 0.0)
    adv = jnp.sum(jnp.where(mine, jnp.concatenate([adv] * copies, axis=1), 0.0), axis=0, keepdims=True)
    hi = ratio.astype(bf16).astype(f32)
    mid = (ratio - hi).astype(bf16).astype(f32)
    low = ratio - hi - mid
    ones = jnp.ones((nt, rows), f32)
    left = jnp.concatenate([hi, mid, low, ones], axis=0).astype(bf16)
    sums = jnp.dot(left, same, preferred_element_type=f32)
    seg_sum = jnp.sum(sums[:3 * nt], axis=0, keepdims=True)
    seg_len = sums[3 * nt:3 * nt + 1]
    weight = jnp.minimum(jnp.exp(seg_sum / seg_len), row_cap)
    live = lax.broadcasted_iota(jnp.int32, (1, rows), 1) < count
    return jnp.where(live, -adv * weight * tokens, 0.0)


def block_kernel(tokens, plane_bits, line_bits, nt, cnt_s,
                 new_hbm, old_hbm, adv_hbm, caps_hbm, seq_hbm, seg_hbm, ver_hbm, q_hbm, k_hbm, v_hbm, g_hbm,
                 dq, dk_ref, dv_ref, coef_ref,
                 q, k, v, g, probs_t, dscore_t, k_t, bias, same, row_cap, dk_sum, dv_sum,
                 caps_s, seq_ref, seg_ref, ver_ref,
                 new_v, old_v, adv_v, own_row, rows_in, cnt_row, cnt_rows, part_row, part_rows,
                 sems, load_sem, send_sem, recv_sem):
    rows, columns = q.shape
    heads = columns // HEAD_DIM
    tiles = rows // TILE
    bf16, f32 = jnp.bfloat16, jnp.float32
    scale = HEAD_DIM ** -0.5
    factor = scale * math.log2(math.e)

    dp = lax.axis_index("dp")
    me = lax.axis_index("tensor")
    owners = partners(me, range(nt.bit_length() - 1))
    tensor_peers = [(dp, t) for t in owners]
    plane_peers = [(d, me) for d in partners(dp, plane_bits)]
    half = nt // 2
    far = me >= half
    across = lax.rem(me + half, nt)
    line_peers = [(d, across) for d in partners(dp, line_bits)]
    cross, beside = tensor_peers[:half], tensor_peers[half:]
    greeted = len(tensor_peers) + len(plane_peers) + len(line_peers)

    barrier = pltpu.get_barrier_semaphore()
    for peer in beside + plane_peers + cross + line_peers:
        pl.semaphore_signal(barrier, inc=1, device_id=peer, device_id_type=MESH)

    def start_all(pairs, sem, first):
        copies = [pltpu.make_async_copy(src, dst, sem.at[first + n]) for n, (src, dst) in enumerate(pairs)]
        for copy in copies:
            copy.start()
        return copies

    def tile_rows(i):
        return pl.ds(i * TILE, TILE)

    own_in = start_all(((new_hbm, new_v), (old_hbm, old_v), (adv_hbm, adv_v)), load_sem, 0)
    small_in = start_all(((seq_hbm, seq_ref), (seg_hbm, seg_ref), (ver_hbm, ver_ref), (caps_hbm, caps_s),
                          (k_hbm, k), (v_hbm, v)), sems, 0)
    wide_in = [start_all(((q_hbm.at[tile_rows(i)], q.at[tile_rows(i)]), (g_hbm.at[tile_rows(i)], g.at[tile_rows(i)])),
                         sems, 6 + 2 * i) for i in range(tiles)]
    def send(src, dst, n, peer):
        pltpu.make_async_remote_copy(
            src_ref=src, dst_ref=dst, send_sem=send_sem.at[n], recv_sem=recv_sem.at[n],
            device_id=peer, device_id_type=MESH).start()

    def drain(buffer, n, sem):
        span = buffer.at[pl.ds(0, n)]
        pltpu.make_async_copy(span, span, sem).wait()

    def send_own():
        for load in own_in:
            load.wait()
        own_row[0] = jnp.concatenate([new_v[...] - old_v[...], adv_v[...]], axis=1)
        cnt_row[0] = jnp.full((1, 128), cnt_s[0].astype(f32), f32)
        pl.semaphore_wait(barrier, greeted)
        for n, peer in enumerate(tensor_peers):
            send(own_row, rows_in.at[pl.ds(n, 1)], 0, peer)
        for n, peer in enumerate(plane_peers):
            send(cnt_row, cnt_rows.at[pl.ds(n, 1)], 1, peer)

    def send_partial():
        drain(cnt_rows, len(plane_peers), recv_sem.at[1])
        part = cnt_row[0]
        for n in range(len(plane_peers)):
            part = part + cnt_rows[n]
        part_row[0] = part
        for n, peer in enumerate(line_peers + [(dp, across)]):
            send(part_row, part_rows.at[pl.ds(n, 1)], 2, peer)

    def head_pair(ref, i, p):
        return jnp.concatenate(
            [ref[i * TILE:(i + 1) * TILE, (2 * p + n) * HEAD_DIM:(2 * p + n + 1) * HEAD_DIM] for n in range(2)],
            axis=0)

    contract_last = (((1,), (1,)), ((), ()))

    @pl.when(far)
    def _():
        send_own()
        send_partial()

    for load in small_in:
        load.wait()
    cap = jnp.zeros((1, rows), f32)
    for n in range(caps_s.shape[0]):
        cap = jnp.where(ver_ref[...] == n, caps_s[n], cap)
    row_cap[...] = cap
    for a, part in enumerate(segment_mask(seg_ref[...])):
        same[:, a * 128:(a + 1) * 128] = part
    k_t[...] = k[...].astype(f32).T.astype(bf16)
    for i in range(tiles):
        span = (i + 1) * TILE
        row_j = lax.broadcasted_iota(jnp.int32, (span, TILE), 0)
        col_t = lax.broadcasted_iota(jnp.int32, (span, TILE), 1) + i * TILE
        begin = seq_ref[:, i * TILE:(i + 1) * TILE]
        bias[0:span, :] = jnp.where((row_j >= begin) & (row_j <= col_t), 0.0, NEG)
        for load in wide_in[i]:
            load.wait()
        for p in range(heads // 2):
            scores = lax.dot_general(k[0:span, :], head_pair(q, i, p), contract_last, preferred_element_type=f32)
            d_prob = lax.dot_general(v[0:span, :], head_pair(g, i, p), contract_last, preferred_element_type=f32)
            scores = scores + jnp.concatenate([bias[0:span, :]] * 2, axis=1)
            top = jnp.max(scores, axis=0, keepdims=True)
            mass = jnp.exp2((scores - top) * factor)
            norm = 1.0 / jnp.sum(mass, axis=0, keepdims=True)
            delta = jnp.sum(mass * d_prob, axis=0, keepdims=True) * norm
            probs = mass * norm
            lanes = slice(i * columns + 2 * p * TILE, i * columns + 2 * (p + 1) * TILE)
            probs_t[0:span, lanes] = probs.astype(bf16)
            dscore_t[0:span, lanes] = (probs * (d_prob - delta)).astype(bf16)
        dq_t = jnp.dot(k_t[:, 0:span], dscore_t[0:span, i * columns:(i + 1) * columns],
                       preferred_element_type=f32) * scale
        for h in range(heads):
            dq[i * TILE:(i + 1) * TILE, h * HEAD_DIM:(h + 1) * HEAD_DIM] = (
                dq_t[:, h * TILE:(h + 1) * TILE].T.astype(bf16))

    @pl.when(jnp.logical_not(far))
    def _():
        send_own()

    drain(rows_in, nt - 1, recv_sem.at[0])
    owner_row = lax.broadcasted_iota(jnp.int32, (nt, 128), 0)
    gathered = jnp.broadcast_to(own_row[0], (nt, 128))
    for n in range(nt - 1):
        gathered = jnp.where(owner_row == owners[n], jnp.broadcast_to(rows_in[n], (nt, 128)), gathered)
    coef = row_coefs(tokens, gathered, same[...], row_cap[...], cnt_s[0])
    coef_col = jnp.broadcast_to(coef, (HEAD_DIM, rows)).T

    def scaled_stack(ref, i):
        here = slice(i * TILE, (i + 1) * TILE)
        return jnp.concatenate(
            [(ref[here, h * HEAD_DIM:(h + 1) * HEAD_DIM].astype(f32) * coef_col[here]).astype(bf16)
             for h in range(heads)], axis=0)

    def stacked_products(source, ref, target):
        for i in reversed(range(tiles)):
            span = (i + 1) * TILE
            part = jnp.dot(source[0:span, i * columns:(i + 1) * columns], scaled_stack(ref, i),
                           preferred_element_type=f32)
            if i == tiles - 1:
                target[...] = part
            else:
                target[0:span, :] = target[0:span, :] + part

    stacked_products(probs_t, g, dv_sum)

    @pl.when(jnp.logical_not(far))
    def _():
        send_partial()

    stacked_products(dscore_t, q, dk_sum)
    drain(part_rows, len(line_peers) + 1, recv_sem.at[2])
    total = part_rows[0]
    for n in range(len(line_peers)):
        total = total + part_rows[n + 1]
    inverse = jnp.where(total > 0.0, 1.0 / total, 0.0)
    coef_ref[...] = coef * jnp.concatenate([inverse] * (rows // 128), axis=1)
    dv_ref[...] = (dv_sum[...] * inverse).astype(bf16)
    dk_ref[...] = (dk_sum[...] * (inverse * scale)).astype(bf16)
    drain(rows_in, nt - 1, send_sem.at[0])
    drain(cnt_rows, len(plane_peers), send_sem.at[1])
    drain(part_rows, len(line_peers) + 1, send_sem.at[2])


def block(tokens, bits, nt, cnt, logp_new, logp_old, advantage, caps, seq_begin, seg_begin, version, q, k, v, g):
    plane_bits, line_bits = bits
    rows, columns = q.shape
    own = logp_new.shape[0]
    tiles = rows // TILE
    planes, low = 1 << len(plane_bits), 1 << len(line_bits)
    bf16, f32, i32 = jnp.bfloat16, jnp.float32, jnp.int32
    hbm = pl.BlockSpec(memory_space=pltpu.HBM)
    vmem = pl.BlockSpec(memory_space=pltpu.VMEM)
    wide, narrow = (rows, columns), (rows, HEAD_DIM)
    dma = pltpu.SemaphoreType.DMA
    return pl.pallas_call(
        functools.partial(block_kernel, tokens, plane_bits, line_bits, nt),
        out_shape=(jax.ShapeDtypeStruct(wide, bf16), jax.ShapeDtypeStruct(narrow, bf16),
                   jax.ShapeDtypeStruct(narrow, bf16), jax.ShapeDtypeStruct((1, rows), f32)),
        in_specs=[pl.BlockSpec(memory_space=pltpu.SMEM)] + [hbm] * 11,
        out_specs=(vmem,) * 4,
        scratch_shapes=[
            pltpu.VMEM(wide, bf16), pltpu.VMEM(narrow, bf16), pltpu.VMEM(narrow, bf16), pltpu.VMEM(wide, bf16),
            pltpu.VMEM((rows, tiles * columns), bf16), pltpu.VMEM((rows, tiles * columns), bf16),
            pltpu.VMEM((HEAD_DIM, rows), bf16), pltpu.VMEM((rows, TILE), f32),
            pltpu.VMEM((rows, rows), bf16), pltpu.VMEM((1, rows), f32),
            pltpu.VMEM(narrow, f32), pltpu.VMEM(narrow, f32),
            pltpu.SMEM(caps.shape, f32),
            pltpu.VMEM((1, rows), i32), pltpu.VMEM((1, rows), i32), pltpu.VMEM((1, rows), i32),
            pltpu.VMEM((1, own), f32), pltpu.VMEM((1, own), f32), pltpu.VMEM((1, own), f32),
            pltpu.VMEM((1, 1, 128), f32), pltpu.VMEM((nt - 1, 1, 128), f32),
            pltpu.VMEM((1, 1, 128), f32), pltpu.VMEM((planes - 1, 1, 128), f32),
            pltpu.VMEM((1, 1, 128), f32), pltpu.VMEM((low, 1, 128), f32),
            dma((6 + 2 * tiles,)), dma((3,)), dma((3,)), dma((3,)),
        ],
        compiler_params=pltpu.CompilerParams(
            collective_id=0, has_side_effects=True, vmem_limit_bytes=32 * 2**20),
        name="block",
    )(cnt, *in_hbm(logp_new.reshape(1, own), logp_old.reshape(1, own), advantage.reshape(1, own), caps,
                   seq_begin.reshape(1, rows), seg_begin.reshape(1, rows), version.reshape(1, rows), q, k, v, g))


def finish_kernel(coef, dq_in, dk_in, dv_in, dq_hbm, dk_hbm, dv_hbm, dq, sems):
    rows, columns = dq.shape
    tiles = rows // TILE
    passed = [pltpu.make_async_copy(dk_in, dk_hbm, sems.at[0]), pltpu.make_async_copy(dv_in, dv_hbm, sems.at[1])]
    stores = [pltpu.make_async_copy(dq.at[pl.ds(i * TILE, TILE)], dq_hbm.at[pl.ds(i * TILE, TILE)], sems.at[2 + i])
              for i in range(tiles)]
    for copy in passed:
        copy.start()
    for i in range(tiles):
        here = slice(i * TILE, (i + 1) * TILE)
        coef_col = jnp.broadcast_to(coef[:, here], (HEAD_DIM, TILE)).T
        for h in range(columns // HEAD_DIM):
            lanes = slice(h * HEAD_DIM, (h + 1) * HEAD_DIM)
            dq[here, lanes] = (dq_in[here, lanes].astype(jnp.float32) * coef_col).astype(dq.dtype)
        stores[i].start()
    for copy in stores + passed:
        copy.wait()


def finish(coef, dq, dk, dv):
    hbm = pl.BlockSpec(memory_space=pltpu.HBM)
    vmem = pl.BlockSpec(memory_space=pltpu.VMEM)
    return pl.pallas_call(
        finish_kernel,
        out_shape=tuple(jax.ShapeDtypeStruct(a.shape, a.dtype) for a in (dq, dk, dv)),
        in_specs=[vmem] * 4,
        out_specs=(hbm,) * 3,
        scratch_shapes=[pltpu.VMEM(dq.shape, dq.dtype), pltpu.SemaphoreType.DMA((2 + dq.shape[0] // TILE,))],
        compiler_params=pltpu.CompilerParams(vmem_limit_bytes=32 * 2**20),
        name="finish",
    )(coef, dq, dk, dv)


def solution(mesh):
    blocks, nt = mesh.shape["dp"], mesh.shape["tensor"]
    top = blocks.bit_length() - 1
    bits = ((0, top - 2, top - 1), tuple(range(1, top - 2)))

    def local(query_heads, key_heads, value_heads, logp_grad, logp_new, logp_old, advantage, ratio_caps,
              live_counts, seq_begin, seg_begin, policy_version):
        tokens = float(query_heads.shape[0] * blocks)
        dq, dk, dv, coef = block(tokens, bits, nt, live_counts, logp_new, logp_old, advantage, ratio_caps,
                                 seq_begin, seg_begin, policy_version, query_heads, key_heads, value_heads, logp_grad)
        return finish(coef, dq, dk, dv)

    row, every = P("dp"), P(("dp", "tensor"))
    both = P("dp", "tensor")
    return jax.shard_map(
        local,
        mesh=mesh,
        in_specs=(both, both, both, both, every, every, every, P(), row, row, row, row),
        out_specs=(both, both, both),
        check_vma=False,
    )
```

```python
import functools
import math

import jax
import jax.numpy as jnp
from jax import lax
from jax.experimental import pallas as pl
from jax.experimental.pallas import tpu as pltpu
from jax.sharding import PartitionSpec as P

HEAD_DIM = 128
TILE = 128
MESH = pl.DeviceIdType.MESH
NEG = -1e30


def in_hbm(*arrays):
    return [pltpu.with_memory_space_constraint(a, pltpu.HBM) for a in arrays]


def flips(index, bits):
    return [(1 << b) * (1 - 2 * lax.rem(lax.div(index, 1 << b), 2)) for b in bits]


def partners(index, bits):
    deltas = flips(index, bits)
    found = []
    for mask in range((1 << len(bits)) - 1, 0, -1):
        other = index
        for n, delta in enumerate(deltas):
            if mask >> n & 1:
                other = other + delta
        found.append(other)
    return found


def segment_mask(seg_row):
    rows = seg_row.shape[1]
    seg = seg_row.astype(jnp.float32)
    seg_col = jnp.broadcast_to(seg, (128, rows)).T
    return [
        jnp.where(seg_col == seg[:, a * 128:(a + 1) * 128], 1.0, 0.0).astype(jnp.bfloat16) for a in range(rows // 128)
    ]


def row_coefs(tokens, gath, same, row_cap, count):
    nt = gath.shape[0]
    rows = row_cap.shape[1]
    half = rows // nt
    bf16, f32 = jnp.bfloat16, jnp.float32
    lane = lax.broadcasted_iota(jnp.int32, (nt, 128), 1)
    other = pltpu.roll(gath, half, 1)
    ratio = jnp.where(lane < half, gath, other)
    adv = jnp.where(lane < half, other, gath)
    place = lax.broadcasted_iota(jnp.int32, (nt, rows), 1) // half
    mine = place == lax.broadcasted_iota(jnp.int32, (nt, rows), 0)
    copies = rows // 128
    ratio = jnp.where(mine, jnp.concatenate([ratio] * copies, axis=1), 0.0)
    adv = jnp.sum(jnp.where(mine, jnp.concatenate([adv] * copies, axis=1), 0.0), axis=0, keepdims=True)
    hi = ratio.astype(bf16).astype(f32)
    mid = (ratio - hi).astype(bf16).astype(f32)
    low = ratio - hi - mid
    ones = jnp.ones((nt, rows), f32)
    left = jnp.concatenate([hi, mid, low, ones], axis=0).astype(bf16)
    sums = jnp.dot(left, same, preferred_element_type=f32)
    seg_sum = jnp.sum(sums[:3 * nt], axis=0, keepdims=True)
    seg_len = sums[3 * nt:3 * nt + 1]
    weight = jnp.minimum(jnp.exp(seg_sum / seg_len), row_cap)
    live = lax.broadcasted_iota(jnp.int32, (1, rows), 1) < count
    return jnp.where(live, -adv * weight * tokens, 0.0)


def block_kernel(tokens, plane_bits, line_bits, nt, cnt_s,
                 new_hbm, old_hbm, adv_hbm, caps_hbm, seq_hbm, seg_hbm, ver_hbm, q_hbm, k_hbm, v_hbm, g_hbm,
                 dq, dk_ref, dv_ref, coef_ref,
                 q, k, v, g, probs_t, dscore_t, k_t, bias, same, row_cap, dk_sum, dv_sum,
                 caps_s, seq_ref, seg_ref, ver_ref,
                 new_v, old_v, adv_v, own_row, rows_in, cnt_row, cnt_rows, part_row, part_rows, total_row,
                 sems, load_sem, send_sem, recv_sem):
    rows, columns = q.shape
    heads = columns // HEAD_DIM
    tiles = rows // TILE
    bf16, f32 = jnp.bfloat16, jnp.float32
    scale = HEAD_DIM ** -0.5
    factor = scale * math.log2(math.e)

    dp = lax.axis_index("dp")
    me = lax.axis_index("tensor")
    owners = partners(me, range(nt.bit_length() - 1))
    tensor_peers = [(dp, t) for t in owners]
    plane_peers = [(d, me) for d in partners(dp, plane_bits)]
    half = nt // 2
    far = me >= half
    across = lax.rem(me + half, nt)
    line_peers = [(d, across) for d in partners(dp, line_bits)]
    cross, beside = tensor_peers[:half], tensor_peers[half:]
    assert nt == len(plane_peers) + 1 == len(line_peers) + 1
    greeted = 2 * (nt - 1)

    barrier = pltpu.get_barrier_semaphore()

    def greet(peers):
        for peer in peers:
            pl.semaphore_signal(barrier, inc=1, device_id=peer, device_id_type=MESH)

    @pl.when(far)
    def _():
        greet(beside + cross)

    @pl.when(jnp.logical_not(far))
    def _():
        greet(cross + line_peers + plane_peers + beside)

    def start_all(pairs, sem, first):
        copies = [pltpu.make_async_copy(src, dst, sem.at[first + n]) for n, (src, dst) in enumerate(pairs)]
        for copy in copies:
            copy.start()
        return copies

    def tile_rows(i):
        return pl.ds(i * TILE, TILE)

    own_in = start_all(((new_hbm, new_v), (old_hbm, old_v), (adv_hbm, adv_v)), load_sem, 0)
    small_in = start_all(((seq_hbm, seq_ref), (seg_hbm, seg_ref), (ver_hbm, ver_ref), (caps_hbm, caps_s),
                          (k_hbm, k), (v_hbm, v)), sems, 0)
    wide_in = [start_all(((q_hbm.at[tile_rows(i)], q.at[tile_rows(i)]), (g_hbm.at[tile_rows(i)], g.at[tile_rows(i)])),
                         sems, 6 + 2 * i) for i in range(tiles)]
    def send(src, dst, n, peer):
        pltpu.make_async_remote_copy(
            src_ref=src, dst_ref=dst, send_sem=send_sem.at[n], recv_sem=recv_sem.at[n],
            device_id=peer, device_id_type=MESH).start()

    def drain(buffer, n, sem):
        span = buffer.at[pl.ds(0, n)]
        pltpu.make_async_copy(span, span, sem).wait()

    def send_rows(first, last):
        for n in range(first, last):
            send(own_row, rows_in.at[pl.ds(n, 1)], 0, tensor_peers[n])

    def ready_to_send():
        for load in own_in:
            load.wait()
        own_row[0] = jnp.concatenate([new_v[...] - old_v[...], adv_v[...]], axis=1)
        pl.semaphore_wait(barrier, greeted)

    def far_sends():
        cnt_row[0] = jnp.full((1, 128), cnt_s[0].astype(f32), f32)
        ready_to_send()
        send_rows(0, half)
        for n, peer in enumerate(line_peers + [(dp, across)]):
            send(cnt_row, cnt_rows.at[pl.ds(n, 1)], 1, peer)
        send_rows(half, nt - 1)

    def send_partial():
        drain(cnt_rows, len(line_peers) + 1, recv_sem.at[1])
        part = cnt_rows[0]
        for n in range(len(line_peers)):
            part = part + cnt_rows[n + 1]
        part_row[0] = part
        for n, peer in enumerate(plane_peers):
            send(part_row, part_rows.at[pl.ds(n, 1)], 2, peer)

    def send_total():
        drain(part_rows, len(plane_peers), recv_sem.at[2])
        total = part_row[0]
        for n in range(len(plane_peers)):
            total = total + part_rows[n]
        total_row[0] = total
        send(total_row, total_row, 3, (dp, across))

    def head_pair(ref, i, p):
        return jnp.concatenate(
            [ref[i * TILE:(i + 1) * TILE, (2 * p + n) * HEAD_DIM:(2 * p + n + 1) * HEAD_DIM] for n in range(2)],
            axis=0)

    contract_last = (((1,), (1,)), ((), ()))

    @pl.when(far)
    def _():
        far_sends()

    for load in small_in:
        load.wait()
    cap = jnp.zeros((1, rows), f32)
    for n in range(caps_s.shape[0]):
        cap = jnp.where(ver_ref[...] == n, caps_s[n], cap)
    row_cap[...] = cap
    for a, part in enumerate(segment_mask(seg_ref[...])):
        same[:, a * 128:(a + 1) * 128] = part
    k_t[...] = k[...].astype(f32).T.astype(bf16)
    for i in range(tiles):
        span = (i + 1) * TILE
        row_j = lax.broadcasted_iota(jnp.int32, (span, TILE), 0)
        col_t = lax.broadcasted_iota(jnp.int32, (span, TILE), 1) + i * TILE
        begin = seq_ref[:, i * TILE:(i + 1) * TILE]
        bias[0:span, :] = jnp.where((row_j >= begin) & (row_j <= col_t), 0.0, NEG)
        for load in wide_in[i]:
            load.wait()
        for p in range(heads // 2):
            scores = lax.dot_general(k[0:span, :], head_pair(q, i, p), contract_last, preferred_element_type=f32)
            d_prob = lax.dot_general(v[0:span, :], head_pair(g, i, p), contract_last, preferred_element_type=f32)
            scores = scores + jnp.concatenate([bias[0:span, :]] * 2, axis=1)
            top = jnp.max(scores, axis=0, keepdims=True)
            mass = jnp.exp2((scores - top) * factor)
            norm = 1.0 / jnp.sum(mass, axis=0, keepdims=True)
            delta = jnp.sum(mass * d_prob, axis=0, keepdims=True) * norm
            probs = mass * norm
            lanes = slice(i * columns + 2 * p * TILE, i * columns + 2 * (p + 1) * TILE)
            probs_t[0:span, lanes] = probs.astype(bf16)
            dscore_t[0:span, lanes] = (probs * (d_prob - delta)).astype(bf16)
        dq_t = jnp.dot(k_t[:, 0:span], dscore_t[0:span, i * columns:(i + 1) * columns],
                       preferred_element_type=f32) * scale
        for h in range(heads):
            dq[i * TILE:(i + 1) * TILE, h * HEAD_DIM:(h + 1) * HEAD_DIM] = (
                dq_t[:, h * TILE:(h + 1) * TILE].T.astype(bf16))

    @pl.when(jnp.logical_not(far))
    def _():
        ready_to_send()
        send_rows(0, nt - 1)

    drain(rows_in, nt - 1, recv_sem.at[0])
    owner_row = lax.broadcasted_iota(jnp.int32, (nt, 128), 0)
    gathered = jnp.broadcast_to(own_row[0], (nt, 128))
    for n in range(nt - 1):
        gathered = jnp.where(owner_row == owners[n], jnp.broadcast_to(rows_in[n], (nt, 128)), gathered)
    coef = row_coefs(tokens, gathered, same[...], row_cap[...], cnt_s[0])
    coef_col = jnp.broadcast_to(coef, (HEAD_DIM, rows)).T

    def scaled_stack(ref, i):
        here = slice(i * TILE, (i + 1) * TILE)
        return jnp.concatenate(
            [(ref[here, h * HEAD_DIM:(h + 1) * HEAD_DIM].astype(f32) * coef_col[here]).astype(bf16)
             for h in range(heads)], axis=0)

    def stacked_products(source, ref, target):
        for i in reversed(range(tiles)):
            span = (i + 1) * TILE
            part = jnp.dot(source[0:span, i * columns:(i + 1) * columns], scaled_stack(ref, i),
                           preferred_element_type=f32)
            if i == tiles - 1:
                target[...] = part
            else:
                target[0:span, :] = target[0:span, :] + part

    @pl.when(jnp.logical_not(far))
    def _():
        send_partial()

    stacked_products(probs_t, g, dv_sum)
    stacked_products(dscore_t, q, dk_sum)

    @pl.when(jnp.logical_not(far))
    def _():
        send_total()

    @pl.when(far)
    def _():
        drain(total_row, 1, recv_sem.at[3])

    total = total_row[0]
    inverse = jnp.where(total > 0.0, 1.0 / total, 0.0)
    coef_ref[...] = coef * jnp.concatenate([inverse] * (rows // 128), axis=1)
    dv_ref[...] = (dv_sum[...] * inverse).astype(bf16)
    dk_ref[...] = (dk_sum[...] * (inverse * scale)).astype(bf16)
    drain(rows_in, nt - 1, send_sem.at[0])

    @pl.when(far)
    def _():
        drain(cnt_rows, len(line_peers) + 1, send_sem.at[1])

    @pl.when(jnp.logical_not(far))
    def _():
        drain(part_rows, len(plane_peers), send_sem.at[2])
        drain(total_row, 1, send_sem.at[3])


def block(tokens, bits, nt, cnt, logp_new, logp_old, advantage, caps, seq_begin, seg_begin, version, q, k, v, g):
    plane_bits, line_bits = bits
    rows, columns = q.shape
    own = logp_new.shape[0]
    tiles = rows // TILE
    planes, low = 1 << len(plane_bits), 1 << len(line_bits)
    bf16, f32, i32 = jnp.bfloat16, jnp.float32, jnp.int32
    hbm = pl.BlockSpec(memory_space=pltpu.HBM)
    vmem = pl.BlockSpec(memory_space=pltpu.VMEM)
    wide, narrow = (rows, columns), (rows, HEAD_DIM)
    dma = pltpu.SemaphoreType.DMA
    return pl.pallas_call(
        functools.partial(block_kernel, tokens, plane_bits, line_bits, nt),
        out_shape=(jax.ShapeDtypeStruct(wide, bf16), jax.ShapeDtypeStruct(narrow, bf16),
                   jax.ShapeDtypeStruct(narrow, bf16), jax.ShapeDtypeStruct((1, rows), f32)),
        in_specs=[pl.BlockSpec(memory_space=pltpu.SMEM)] + [hbm] * 11,
        out_specs=(vmem,) * 4,
        scratch_shapes=[
            pltpu.VMEM(wide, bf16), pltpu.VMEM(narrow, bf16), pltpu.VMEM(narrow, bf16), pltpu.VMEM(wide, bf16),
            pltpu.VMEM((rows, tiles * columns), bf16), pltpu.VMEM((rows, tiles * columns), bf16),
            pltpu.VMEM((HEAD_DIM, rows), bf16), pltpu.VMEM((rows, TILE), f32),
            pltpu.VMEM((rows, rows), bf16), pltpu.VMEM((1, rows), f32),
            pltpu.VMEM(narrow, f32), pltpu.VMEM(narrow, f32),
            pltpu.SMEM(caps.shape, f32),
            pltpu.VMEM((1, rows), i32), pltpu.VMEM((1, rows), i32), pltpu.VMEM((1, rows), i32),
            pltpu.VMEM((1, own), f32), pltpu.VMEM((1, own), f32), pltpu.VMEM((1, own), f32),
            pltpu.VMEM((1, 1, 128), f32), pltpu.VMEM((nt - 1, 1, 128), f32),
            pltpu.VMEM((1, 1, 128), f32), pltpu.VMEM((low, 1, 128), f32),
            pltpu.VMEM((1, 1, 128), f32), pltpu.VMEM((planes - 1, 1, 128), f32), pltpu.VMEM((1, 1, 128), f32),
            dma((6 + 2 * tiles,)), dma((3,)), dma((4,)), dma((4,)),
        ],
        compiler_params=pltpu.CompilerParams(
            collective_id=0, has_side_effects=True, vmem_limit_bytes=32 * 2**20),
        name="block",
    )(cnt, *in_hbm(logp_new.reshape(1, own), logp_old.reshape(1, own), advantage.reshape(1, own), caps,
                   seq_begin.reshape(1, rows), seg_begin.reshape(1, rows), version.reshape(1, rows), q, k, v, g))


def finish_kernel(coef, dq_in, dk_in, dv_in, dq_hbm, dk_hbm, dv_hbm, dq, sems):
    rows, columns = dq.shape
    tiles = rows // TILE
    passed = [pltpu.make_async_copy(dk_in, dk_hbm, sems.at[0]), pltpu.make_async_copy(dv_in, dv_hbm, sems.at[1])]
    stores = [pltpu.make_async_copy(dq.at[pl.ds(i * TILE, TILE)], dq_hbm.at[pl.ds(i * TILE, TILE)], sems.at[2 + i])
              for i in range(tiles)]
    for copy in passed:
        copy.start()
    for i in range(tiles):
        here = slice(i * TILE, (i + 1) * TILE)
        coef_col = jnp.broadcast_to(coef[:, here], (HEAD_DIM, TILE)).T
        for h in range(columns // HEAD_DIM):
            lanes = slice(h * HEAD_DIM, (h + 1) * HEAD_DIM)
            dq[here, lanes] = (dq_in[here, lanes].astype(jnp.float32) * coef_col).astype(dq.dtype)
        stores[i].start()
    for copy in stores + passed:
        copy.wait()


def finish(coef, dq, dk, dv):
    hbm = pl.BlockSpec(memory_space=pltpu.HBM)
    vmem = pl.BlockSpec(memory_space=pltpu.VMEM)
    return pl.pallas_call(
        finish_kernel,
        out_shape=tuple(jax.ShapeDtypeStruct(a.shape, a.dtype) for a in (dq, dk, dv)),
        in_specs=[vmem] * 4,
        out_specs=(hbm,) * 3,
        scratch_shapes=[pltpu.VMEM(dq.shape, dq.dtype), pltpu.SemaphoreType.DMA((2 + dq.shape[0] // TILE,))],
        compiler_params=pltpu.CompilerParams(vmem_limit_bytes=32 * 2**20),
        name="finish",
    )(coef, dq, dk, dv)


def solution(mesh):
    blocks, nt = mesh.shape["dp"], mesh.shape["tensor"]
    top = blocks.bit_length() - 1
    bits = ((0, top - 2, top - 1), tuple(range(1, top - 2)))

    def local(query_heads, key_heads, value_heads, logp_grad, logp_new, logp_old, advantage, ratio_caps,
              live_counts, seq_begin, seg_begin, policy_version):
        tokens = float(query_heads.shape[0] * blocks)
        dq, dk, dv, coef = block(tokens, bits, nt, live_counts, logp_new, logp_old, advantage, ratio_caps,
                                 seq_begin, seg_begin, policy_version, query_heads, key_heads, value_heads, logp_grad)
        return finish(coef, dq, dk, dv)

    row, every = P("dp"), P(("dp", "tensor"))
    both = P("dp", "tensor")
    return jax.shard_map(
        local,
        mesh=mesh,
        in_specs=(both, both, both, both, every, every, every, P(), row, row, row, row),
        out_specs=(both, both, both),
        check_vma=False,
    )
```

```python
import functools
import math

import jax
import jax.numpy as jnp
from jax import lax
from jax.experimental import pallas as pl
from jax.experimental.pallas import tpu as pltpu
from jax.sharding import PartitionSpec as P

HEAD_DIM = 128
TILE = 128
MESH = pl.DeviceIdType.MESH
NEG = -1e30


def in_hbm(*arrays):
    return [pltpu.with_memory_space_constraint(a, pltpu.HBM) for a in arrays]


def flips(index, bits):
    return [(1 << b) * (1 - 2 * lax.rem(lax.div(index, 1 << b), 2)) for b in bits]


def partners(index, bits):
    deltas = flips(index, bits)
    found = []
    for mask in range((1 << len(bits)) - 1, 0, -1):
        other = index
        for n, delta in enumerate(deltas):
            if mask >> n & 1:
                other = other + delta
        found.append(other)
    return found


def segment_mask(seg_row):
    rows = seg_row.shape[1]
    seg = seg_row.astype(jnp.float32)
    seg_col = jnp.broadcast_to(seg, (128, rows)).T
    return [
        jnp.where(seg_col == seg[:, a * 128:(a + 1) * 128], 1.0, 0.0).astype(jnp.bfloat16) for a in range(rows // 128)
    ]


def row_coefs(tokens, gath, same, row_cap, count):
    nt = gath.shape[0]
    rows = row_cap.shape[1]
    half = rows // nt
    bf16, f32 = jnp.bfloat16, jnp.float32
    lane = lax.broadcasted_iota(jnp.int32, (nt, 128), 1)
    other = pltpu.roll(gath, half, 1)
    ratio = jnp.where(lane < half, gath, other)
    adv = jnp.where(lane < half, other, gath)
    place = lax.broadcasted_iota(jnp.int32, (nt, rows), 1) // half
    mine = place == lax.broadcasted_iota(jnp.int32, (nt, rows), 0)
    copies = rows // 128
    ratio = jnp.where(mine, jnp.concatenate([ratio] * copies, axis=1), 0.0)
    adv = jnp.sum(jnp.where(mine, jnp.concatenate([adv] * copies, axis=1), 0.0), axis=0, keepdims=True)
    hi = ratio.astype(bf16).astype(f32)
    mid = (ratio - hi).astype(bf16).astype(f32)
    low = ratio - hi - mid
    ones = jnp.ones((nt, rows), f32)
    left = jnp.concatenate([hi, mid, low, ones], axis=0).astype(bf16)
    sums = jnp.dot(left, same, preferred_element_type=f32)
    seg_sum = jnp.sum(sums[:3 * nt], axis=0, keepdims=True)
    seg_len = sums[3 * nt:3 * nt + 1]
    weight = jnp.minimum(jnp.exp(seg_sum / seg_len), row_cap)
    live = lax.broadcasted_iota(jnp.int32, (1, rows), 1) < count
    return jnp.where(live, -adv * weight * tokens, 0.0)


def block_kernel(tokens, plane_bits, line_bits, nt, cnt_s,
                 new_hbm, old_hbm, adv_hbm, caps_hbm, seq_hbm, seg_hbm, ver_hbm, q_hbm, k_hbm, v_hbm, g_hbm,
                 dq, dk_ref, dv_ref, coef_ref,
                 q, k, v, g, probs_t, dscore_t, k_t, bias, same, row_cap, dk_sum, dv_sum,
                 caps_s, seq_ref, seg_ref, ver_ref,
                 new_v, old_v, adv_v, own_row, rows_in, cnt_row, cnt_rows, part_row, part_rows,
                 sems, load_sem, send_sem, recv_sem):
    rows, columns = q.shape
    heads = columns // HEAD_DIM
    tiles = rows // TILE
    bf16, f32 = jnp.bfloat16, jnp.float32
    scale = HEAD_DIM ** -0.5
    factor = scale * math.log2(math.e)

    dp = lax.axis_index("dp")
    me = lax.axis_index("tensor")
    owners = partners(me, range(nt.bit_length() - 1))
    tensor_peers = [(dp, t) for t in owners]
    plane_peers = [(d, me) for d in partners(dp, plane_bits)]
    half = nt // 2
    far = me >= half
    across = lax.rem(me + half, nt)
    line_peers = [(d, across) for d in partners(dp, line_bits)]
    cross, beside = tensor_peers[:half], tensor_peers[half:]
    greeted = len(tensor_peers) + len(plane_peers) + len(line_peers)

    barrier = pltpu.get_barrier_semaphore()
    for peer in beside + plane_peers + cross + line_peers:
        pl.semaphore_signal(barrier, inc=1, device_id=peer, device_id_type=MESH)

    def start_all(pairs, sem, first):
        copies = [pltpu.make_async_copy(src, dst, sem.at[first + n]) for n, (src, dst) in enumerate(pairs)]
        for copy in copies:
            copy.start()
        return copies

    def tile_rows(i):
        return pl.ds(i * TILE, TILE)

    own_in = start_all(((new_hbm, new_v), (old_hbm, old_v), (adv_hbm, adv_v)), load_sem, 0)
    small_in = start_all(((seq_hbm, seq_ref), (seg_hbm, seg_ref), (ver_hbm, ver_ref), (caps_hbm, caps_s),
                          (k_hbm, k), (v_hbm, v)), sems, 0)
    wide_in = [start_all(((q_hbm.at[tile_rows(i)], q.at[tile_rows(i)]), (g_hbm.at[tile_rows(i)], g.at[tile_rows(i)])),
                         sems, 6 + 2 * i) for i in range(tiles)]
    def send(src, dst, n, peer):
        pltpu.make_async_remote_copy(
            src_ref=src, dst_ref=dst, send_sem=send_sem.at[n], recv_sem=recv_sem.at[n],
            device_id=peer, device_id_type=MESH).start()

    def drain(buffer, n, sem):
        span = buffer.at[pl.ds(0, n)]
        pltpu.make_async_copy(span, span, sem).wait()

    def send_rows(first, last):
        for n in range(first, last):
            send(own_row, rows_in.at[pl.ds(n, 1)], 0, tensor_peers[n])

    def send_own():
        for load in own_in:
            load.wait()
        own_row[0] = jnp.concatenate([new_v[...] - old_v[...], adv_v[...]], axis=1)
        cnt_row[0] = jnp.full((1, 128), cnt_s[0].astype(f32), f32)
        pl.semaphore_wait(barrier, greeted)
        send_rows(0, half)
        for n, peer in enumerate(plane_peers):
            send(cnt_row, cnt_rows.at[pl.ds(n, 1)], 1, peer)
        send_rows(half, nt - 1)

    def send_partial():
        drain(cnt_rows, len(plane_peers), recv_sem.at[1])
        part = cnt_row[0]
        for n in range(len(plane_peers)):
            part = part + cnt_rows[n]
        part_row[0] = part
        for n, peer in enumerate(line_peers + [(dp, across)]):
            send(part_row, part_rows.at[pl.ds(n, 1)], 2, peer)

    def head_pair(ref, i, p):
        return jnp.concatenate(
            [ref[i * TILE:(i + 1) * TILE, (2 * p + n) * HEAD_DIM:(2 * p + n + 1) * HEAD_DIM] for n in range(2)],
            axis=0)

    contract_last = (((1,), (1,)), ((), ()))

    @pl.when(far)
    def _():
        send_own()
        send_partial()

    for load in small_in:
        load.wait()
    cap = jnp.zeros((1, rows), f32)
    for n in range(caps_s.shape[0]):
        cap = jnp.where(ver_ref[...] == n, caps_s[n], cap)
    row_cap[...] = cap
    for a, part in enumerate(segment_mask(seg_ref[...])):
        same[:, a * 128:(a + 1) * 128] = part
    k_t[...] = k[...].astype(f32).T.astype(bf16)
    for i in range(tiles):
        span = (i + 1) * TILE
        row_j = lax.broadcasted_iota(jnp.int32, (span, TILE), 0)
        col_t = lax.broadcasted_iota(jnp.int32, (span, TILE), 1) + i * TILE
        begin = seq_ref[:, i * TILE:(i + 1) * TILE]
        bias[0:span, :] = jnp.where((row_j >= begin) & (row_j <= col_t), 0.0, NEG)
        for load in wide_in[i]:
            load.wait()
        for p in range(heads // 2):
            scores = lax.dot_general(k[0:span, :], head_pair(q, i, p), contract_last, preferred_element_type=f32)
            d_prob = lax.dot_general(v[0:span, :], head_pair(g, i, p), contract_last, preferred_element_type=f32)
            scores = scores + jnp.concatenate([bias[0:span, :]] * 2, axis=1)
            top = jnp.max(scores, axis=0, keepdims=True)
            mass = jnp.exp2((scores - top) * factor)
            norm = 1.0 / jnp.sum(mass, axis=0, keepdims=True)
            delta = jnp.sum(mass * d_prob, axis=0, keepdims=True) * norm
            probs = mass * norm
            lanes = slice(i * columns + 2 * p * TILE, i * columns + 2 * (p + 1) * TILE)
            probs_t[0:span, lanes] = probs.astype(bf16)
            dscore_t[0:span, lanes] = (probs * (d_prob - delta)).astype(bf16)
        dq_t = jnp.dot(k_t[:, 0:span], dscore_t[0:span, i * columns:(i + 1) * columns],
                       preferred_element_type=f32) * scale
        for h in range(heads):
            dq[i * TILE:(i + 1) * TILE, h * HEAD_DIM:(h + 1) * HEAD_DIM] = (
                dq_t[:, h * TILE:(h + 1) * TILE].T.astype(bf16))

    @pl.when(jnp.logical_not(far))
    def _():
        send_own()
        send_partial()

    drain(rows_in, nt - 1, recv_sem.at[0])
    owner_row = lax.broadcasted_iota(jnp.int32, (nt, 128), 0)
    gathered = jnp.broadcast_to(own_row[0], (nt, 128))
    for n in range(nt - 1):
        gathered = jnp.where(owner_row == owners[n], jnp.broadcast_to(rows_in[n], (nt, 128)), gathered)
    coef = row_coefs(tokens, gathered, same[...], row_cap[...], cnt_s[0])
    coef_col = jnp.broadcast_to(coef, (HEAD_DIM, rows)).T

    def scaled_stack(ref, i):
        here = slice(i * TILE, (i + 1) * TILE)
        return jnp.concatenate(
            [(ref[here, h * HEAD_DIM:(h + 1) * HEAD_DIM].astype(f32) * coef_col[here]).astype(bf16)
             for h in range(heads)], axis=0)

    def stacked_products(source, ref, target):
        for i in reversed(range(tiles)):
            span = (i + 1) * TILE
            part = jnp.dot(source[0:span, i * columns:(i + 1) * columns], scaled_stack(ref, i),
                           preferred_element_type=f32)
            if i == tiles - 1:
                target[...] = part
            else:
                target[0:span, :] = target[0:span, :] + part

    stacked_products(probs_t, g, dv_sum)
    stacked_products(dscore_t, q, dk_sum)
    drain(part_rows, len(line_peers) + 1, recv_sem.at[2])
    total = part_rows[0]
    for n in range(len(line_peers)):
        total = total + part_rows[n + 1]
    inverse = jnp.where(total > 0.0, 1.0 / total, 0.0)
    coef_ref[...] = coef * jnp.concatenate([inverse] * (rows // 128), axis=1)
    dv_ref[...] = (dv_sum[...] * inverse).astype(bf16)
    dk_ref[...] = (dk_sum[...] * (inverse * scale)).astype(bf16)
    drain(rows_in, nt - 1, send_sem.at[0])
    drain(cnt_rows, len(plane_peers), send_sem.at[1])
    drain(part_rows, len(line_peers) + 1, send_sem.at[2])


def block(tokens, bits, nt, cnt, logp_new, logp_old, advantage, caps, seq_begin, seg_begin, version, q, k, v, g):
    plane_bits, line_bits = bits
    rows, columns = q.shape
    own = logp_new.shape[0]
    tiles = rows // TILE
    planes, low = 1 << len(plane_bits), 1 << len(line_bits)
    bf16, f32, i32 = jnp.bfloat16, jnp.float32, jnp.int32
    hbm = pl.BlockSpec(memory_space=pltpu.HBM)
    vmem = pl.BlockSpec(memory_space=pltpu.VMEM)
    wide, narrow = (rows, columns), (rows, HEAD_DIM)
    dma = pltpu.SemaphoreType.DMA
    return pl.pallas_call(
        functools.partial(block_kernel, tokens, plane_bits, line_bits, nt),
        out_shape=(jax.ShapeDtypeStruct(wide, bf16), jax.ShapeDtypeStruct(narrow, bf16),
                   jax.ShapeDtypeStruct(narrow, bf16), jax.ShapeDtypeStruct((1, rows), f32)),
        in_specs=[pl.BlockSpec(memory_space=pltpu.SMEM)] + [hbm] * 11,
        out_specs=(vmem,) * 4,
        scratch_shapes=[
            pltpu.VMEM(wide, bf16), pltpu.VMEM(narrow, bf16), pltpu.VMEM(narrow, bf16), pltpu.VMEM(wide, bf16),
            pltpu.VMEM((rows, tiles * columns), bf16), pltpu.VMEM((rows, tiles * columns), bf16),
            pltpu.VMEM((HEAD_DIM, rows), bf16), pltpu.VMEM((rows, TILE), f32),
            pltpu.VMEM((rows, rows), bf16), pltpu.VMEM((1, rows), f32),
            pltpu.VMEM(narrow, f32), pltpu.VMEM(narrow, f32),
            pltpu.SMEM(caps.shape, f32),
            pltpu.VMEM((1, rows), i32), pltpu.VMEM((1, rows), i32), pltpu.VMEM((1, rows), i32),
            pltpu.VMEM((1, own), f32), pltpu.VMEM((1, own), f32), pltpu.VMEM((1, own), f32),
            pltpu.VMEM((1, 1, 128), f32), pltpu.VMEM((nt - 1, 1, 128), f32),
            pltpu.VMEM((1, 1, 128), f32), pltpu.VMEM((planes - 1, 1, 128), f32),
            pltpu.VMEM((1, 1, 128), f32), pltpu.VMEM((low, 1, 128), f32),
            dma((6 + 2 * tiles,)), dma((3,)), dma((3,)), dma((3,)),
        ],
        compiler_params=pltpu.CompilerParams(
            collective_id=0, has_side_effects=True, vmem_limit_bytes=32 * 2**20),
        name="block",
    )(cnt, *in_hbm(logp_new.reshape(1, own), logp_old.reshape(1, own), advantage.reshape(1, own), caps,
                   seq_begin.reshape(1, rows), seg_begin.reshape(1, rows), version.reshape(1, rows), q, k, v, g))


def finish_kernel(coef, dq_in, dk_in, dv_in, dq_hbm, dk_hbm, dv_hbm, dq, sems):
    rows, columns = dq.shape
    tiles = rows // TILE
    passed = [pltpu.make_async_copy(dk_in, dk_hbm, sems.at[0]), pltpu.make_async_copy(dv_in, dv_hbm, sems.at[1])]
    stores = [pltpu.make_async_copy(dq.at[pl.ds(i * TILE, TILE)], dq_hbm.at[pl.ds(i * TILE, TILE)], sems.at[2 + i])
              for i in range(tiles)]
    for copy in passed:
        copy.start()
    for i in range(tiles):
        here = slice(i * TILE, (i + 1) * TILE)
        coef_col = jnp.broadcast_to(coef[:, here], (HEAD_DIM, TILE)).T
        for h in range(columns // HEAD_DIM):
            lanes = slice(h * HEAD_DIM, (h + 1) * HEAD_DIM)
            dq[here, lanes] = (dq_in[here, lanes].astype(jnp.float32) * coef_col).astype(dq.dtype)
        stores[i].start()
    for copy in stores + passed:
        copy.wait()


def finish(coef, dq, dk, dv):
    hbm = pl.BlockSpec(memory_space=pltpu.HBM)
    vmem = pl.BlockSpec(memory_space=pltpu.VMEM)
    return pl.pallas_call(
        finish_kernel,
        out_shape=tuple(jax.ShapeDtypeStruct(a.shape, a.dtype) for a in (dq, dk, dv)),
        in_specs=[vmem] * 4,
        out_specs=(hbm,) * 3,
        scratch_shapes=[pltpu.VMEM(dq.shape, dq.dtype), pltpu.SemaphoreType.DMA((2 + dq.shape[0] // TILE,))],
        compiler_params=pltpu.CompilerParams(vmem_limit_bytes=32 * 2**20),
        name="finish",
    )(coef, dq, dk, dv)


def solution(mesh):
    blocks, nt = mesh.shape["dp"], mesh.shape["tensor"]
    top = blocks.bit_length() - 1
    bits = ((0,), tuple(range(1, top)))

    def local(query_heads, key_heads, value_heads, logp_grad, logp_new, logp_old, advantage, ratio_caps,
              live_counts, seq_begin, seg_begin, policy_version):
        tokens = float(query_heads.shape[0] * blocks)
        dq, dk, dv, coef = block(tokens, bits, nt, live_counts, logp_new, logp_old, advantage, ratio_caps,
                                 seq_begin, seg_begin, policy_version, query_heads, key_heads, value_heads, logp_grad)
        return finish(coef, dq, dk, dv)

    row, every = P("dp"), P(("dp", "tensor"))
    both = P("dp", "tensor")
    return jax.shard_map(
        local,
        mesh=mesh,
        in_specs=(both, both, both, both, every, every, every, P(), row, row, row, row),
        out_specs=(both, both, both),
        check_vma=False,
    )
```

```python
import functools
import math

import jax
import jax.numpy as jnp
from jax import lax
from jax.experimental import pallas as pl
from jax.experimental.pallas import tpu as pltpu
from jax.sharding import PartitionSpec as P

HEAD_DIM = 128
TILE = 128
MESH = pl.DeviceIdType.MESH
NEG = -1e30


def in_hbm(*arrays):
    return [pltpu.with_memory_space_constraint(a, pltpu.HBM) for a in arrays]


def flips(index, bits):
    return [(1 << b) * (1 - 2 * lax.rem(lax.div(index, 1 << b), 2)) for b in bits]


def partners(index, bits):
    deltas = flips(index, bits)
    found = []
    for mask in range((1 << len(bits)) - 1, 0, -1):
        other = index
        for n, delta in enumerate(deltas):
            if mask >> n & 1:
                other = other + delta
        found.append(other)
    return found


def segment_mask(seg_row):
    rows = seg_row.shape[1]
    seg = seg_row.astype(jnp.float32)
    seg_col = jnp.broadcast_to(seg, (128, rows)).T
    return [
        jnp.where(seg_col == seg[:, a * 128:(a + 1) * 128], 1.0, 0.0).astype(jnp.bfloat16) for a in range(rows // 128)
    ]


def row_coefs(tokens, gath, same, row_cap, count):
    nt = gath.shape[0]
    rows = row_cap.shape[1]
    half = rows // nt
    bf16, f32 = jnp.bfloat16, jnp.float32
    lane = lax.broadcasted_iota(jnp.int32, (nt, 128), 1)
    other = pltpu.roll(gath, half, 1)
    ratio = jnp.where(lane < half, gath, other)
    adv = jnp.where(lane < half, other, gath)
    place = lax.broadcasted_iota(jnp.int32, (nt, rows), 1) // half
    mine = place == lax.broadcasted_iota(jnp.int32, (nt, rows), 0)
    copies = rows // 128
    ratio = jnp.where(mine, jnp.concatenate([ratio] * copies, axis=1), 0.0)
    adv = jnp.sum(jnp.where(mine, jnp.concatenate([adv] * copies, axis=1), 0.0), axis=0, keepdims=True)
    hi = ratio.astype(bf16).astype(f32)
    mid = (ratio - hi).astype(bf16).astype(f32)
    low = ratio - hi - mid
    ones = jnp.ones((nt, rows), f32)
    left = jnp.concatenate([hi, mid, low, ones], axis=0).astype(bf16)
    sums = jnp.dot(left, same, preferred_element_type=f32)
    seg_sum = jnp.sum(sums[:3 * nt], axis=0, keepdims=True)
    seg_len = sums[3 * nt:3 * nt + 1]
    weight = jnp.minimum(jnp.exp(seg_sum / seg_len), row_cap)
    live = lax.broadcasted_iota(jnp.int32, (1, rows), 1) < count
    return jnp.where(live, -adv * weight * tokens, 0.0)


def block_kernel(tokens, bits, nt, cnt_s,
                 new_hbm, old_hbm, adv_hbm, caps_hbm, seq_hbm, seg_hbm, ver_hbm, q_hbm, k_hbm, v_hbm, g_hbm,
                 dq, dk_ref, dv_ref, coef_ref,
                 q, k, v, g, probs_t, dscore_t, k_t, bias, same, row_cap, dk_sum, dv_sum,
                 caps_s, seq_ref, seg_ref, ver_ref,
                 new_v, old_v, adv_v, own_row, rows_in, cnt_row, cnt_rows, part_row, part_rows, total_row,
                 sems, load_sem, send_sem, recv_sem):
    rows, columns = q.shape
    heads = columns // HEAD_DIM
    tiles = rows // TILE
    bf16, f32 = jnp.bfloat16, jnp.float32
    scale = HEAD_DIM ** -0.5
    factor = scale * math.log2(math.e)

    dp = lax.axis_index("dp")
    me = lax.axis_index("tensor")
    owners = partners(me, range(nt.bit_length() - 1))
    tensor_peers = [(dp, t) for t in owners]
    half = nt // 2
    far = me >= half
    near = jnp.logical_not(far)
    across = lax.rem(me + half, nt)
    cross, beside = tensor_peers[:half], tensor_peers[half:]
    own_cross = [(dp, across)]
    far_bits, near_bits = bits
    far_plane, near_plane = ([(d, me) for d in partners(dp, part[0])] for part in (far_bits, near_bits))
    far_line, near_line = ([(d, across) for d in partners(dp, part[1])] for part in (far_bits, near_bits))

    barrier = pltpu.get_barrier_semaphore()

    def greet(peers):
        for peer in peers:
            pl.semaphore_signal(barrier, inc=1, device_id=peer, device_id_type=MESH)

    @pl.when(far)
    def _():
        greet(beside + far_plane + cross + near_line)

    @pl.when(near)
    def _():
        greet(cross + far_line + near_plane + beside)

    def start_all(pairs, sem, first):
        copies = [pltpu.make_async_copy(src, dst, sem.at[first + n]) for n, (src, dst) in enumerate(pairs)]
        for copy in copies:
            copy.start()
        return copies

    def tile_rows(i):
        return pl.ds(i * TILE, TILE)

    own_in = start_all(((new_hbm, new_v), (old_hbm, old_v), (adv_hbm, adv_v)), load_sem, 0)
    small_in = start_all(((seq_hbm, seq_ref), (seg_hbm, seg_ref), (ver_hbm, ver_ref), (caps_hbm, caps_s),
                          (k_hbm, k), (v_hbm, v)), sems, 0)
    wide_in = [start_all(((q_hbm.at[tile_rows(i)], q.at[tile_rows(i)]), (g_hbm.at[tile_rows(i)], g.at[tile_rows(i)])),
                         sems, 6 + 2 * i) for i in range(tiles)]
    def send(src, dst, n, peer):
        pltpu.make_async_remote_copy(
            src_ref=src, dst_ref=dst, send_sem=send_sem.at[n], recv_sem=recv_sem.at[n],
            device_id=peer, device_id_type=MESH).start()

    def drain(buffer, n, sem):
        span = buffer.at[pl.ds(0, n)]
        pltpu.make_async_copy(span, span, sem).wait()

    def send_rows(first, last):
        for n in range(first, last):
            send(own_row, rows_in.at[pl.ds(n, 1)], 0, tensor_peers[n])

    def send_own(plane, line):
        for load in own_in:
            load.wait()
        own_row[0] = jnp.concatenate([new_v[...] - old_v[...], adv_v[...]], axis=1)
        cnt_row[0] = jnp.full((1, 128), cnt_s[0].astype(f32), f32)
        pl.semaphore_wait(barrier, nt - 1 + len(plane) + len(line))
        send_rows(0, half)
        for n, peer in enumerate(plane):
            send(cnt_row, cnt_rows.at[pl.ds(n, 1)], 1, peer)
        send_rows(half, nt - 1)

    def send_partial(plane, line):
        drain(cnt_rows, len(plane), recv_sem.at[1])
        part = cnt_row[0]
        for n in range(len(plane)):
            part = part + cnt_rows[n]
        part_row[0] = part
        for n, peer in enumerate(line + own_cross):
            send(part_row, part_rows.at[pl.ds(n, 1)], 2, peer)

    def sum_total(line):
        drain(part_rows, len(line) + 1, recv_sem.at[2])
        total = part_rows[0]
        for n in range(len(line)):
            total = total + part_rows[n + 1]
        total_row[0] = total

    def drain_sends(plane, line):
        drain(cnt_rows, len(plane), send_sem.at[1])
        drain(part_rows, len(line) + 1, send_sem.at[2])

    def head_pair(ref, i, p):
        return jnp.concatenate(
            [ref[i * TILE:(i + 1) * TILE, (2 * p + n) * HEAD_DIM:(2 * p + n + 1) * HEAD_DIM] for n in range(2)],
            axis=0)

    contract_last = (((1,), (1,)), ((), ()))

    @pl.when(far)
    def _():
        send_own(far_plane, far_line)
        send_partial(far_plane, far_line)

    for load in small_in:
        load.wait()
    cap = jnp.zeros((1, rows), f32)
    for n in range(caps_s.shape[0]):
        cap = jnp.where(ver_ref[...] == n, caps_s[n], cap)
    row_cap[...] = cap
    for a, part in enumerate(segment_mask(seg_ref[...])):
        same[:, a * 128:(a + 1) * 128] = part
    k_t[...] = k[...].astype(f32).T.astype(bf16)
    for i in range(tiles):
        span = (i + 1) * TILE
        row_j = lax.broadcasted_iota(jnp.int32, (span, TILE), 0)
        col_t = lax.broadcasted_iota(jnp.int32, (span, TILE), 1) + i * TILE
        begin = seq_ref[:, i * TILE:(i + 1) * TILE]
        bias[0:span, :] = jnp.where((row_j >= begin) & (row_j <= col_t), 0.0, NEG)
        for load in wide_in[i]:
            load.wait()
        for p in range(heads // 2):
            scores = lax.dot_general(k[0:span, :], head_pair(q, i, p), contract_last, preferred_element_type=f32)
            d_prob = lax.dot_general(v[0:span, :], head_pair(g, i, p), contract_last, preferred_element_type=f32)
            scores = scores + jnp.concatenate([bias[0:span, :]] * 2, axis=1)
            top = jnp.max(scores, axis=0, keepdims=True)
            mass = jnp.exp2((scores - top) * factor)
            norm = 1.0 / jnp.sum(mass, axis=0, keepdims=True)
            delta = jnp.sum(mass * d_prob, axis=0, keepdims=True) * norm
            probs = mass * norm
            lanes = slice(i * columns + 2 * p * TILE, i * columns + 2 * (p + 1) * TILE)
            probs_t[0:span, lanes] = probs.astype(bf16)
            dscore_t[0:span, lanes] = (probs * (d_prob - delta)).astype(bf16)
        dq_t = jnp.dot(k_t[:, 0:span], dscore_t[0:span, i * columns:(i + 1) * columns],
                       preferred_element_type=f32) * scale
        for h in range(heads):
            dq[i * TILE:(i + 1) * TILE, h * HEAD_DIM:(h + 1) * HEAD_DIM] = (
                dq_t[:, h * TILE:(h + 1) * TILE].T.astype(bf16))

    @pl.when(near)
    def _():
        send_own(near_plane, near_line)

    drain(rows_in, nt - 1, recv_sem.at[0])
    owner_row = lax.broadcasted_iota(jnp.int32, (nt, 128), 0)
    gathered = jnp.broadcast_to(own_row[0], (nt, 128))
    for n in range(nt - 1):
        gathered = jnp.where(owner_row == owners[n], jnp.broadcast_to(rows_in[n], (nt, 128)), gathered)
    coef = row_coefs(tokens, gathered, same[...], row_cap[...], cnt_s[0])
    coef_col = jnp.broadcast_to(coef, (HEAD_DIM, rows)).T

    def scaled_stack(ref, i):
        here = slice(i * TILE, (i + 1) * TILE)
        return jnp.concatenate(
            [(ref[here, h * HEAD_DIM:(h + 1) * HEAD_DIM].astype(f32) * coef_col[here]).astype(bf16)
             for h in range(heads)], axis=0)

    def stacked_products(source, ref, target):
        for i in reversed(range(tiles)):
            span = (i + 1) * TILE
            part = jnp.dot(source[0:span, i * columns:(i + 1) * columns], scaled_stack(ref, i),
                           preferred_element_type=f32)
            if i == tiles - 1:
                target[...] = part
            else:
                target[0:span, :] = target[0:span, :] + part

    stacked_products(probs_t, g, dv_sum)

    @pl.when(near)
    def _():
        send_partial(near_plane, near_line)

    stacked_products(dscore_t, q, dk_sum)

    @pl.when(near)
    def _():
        sum_total(far_line)

    @pl.when(far)
    def _():
        sum_total(near_line)

    total = total_row[0]
    inverse = jnp.where(total > 0.0, 1.0 / total, 0.0)
    coef_ref[...] = coef * jnp.concatenate([inverse] * (rows // 128), axis=1)
    dv_ref[...] = (dv_sum[...] * inverse).astype(bf16)
    dk_ref[...] = (dk_sum[...] * (inverse * scale)).astype(bf16)
    drain(rows_in, nt - 1, send_sem.at[0])

    @pl.when(far)
    def _():
        drain_sends(far_plane, far_line)

    @pl.when(near)
    def _():
        drain_sends(near_plane, near_line)


def block(tokens, bits, nt, cnt, logp_new, logp_old, advantage, caps, seq_begin, seg_begin, version, q, k, v, g):
    rows, columns = q.shape
    own = logp_new.shape[0]
    tiles = rows // TILE
    planes, low = 1 << max(len(part[0]) for part in bits), 1 << max(len(part[1]) for part in bits)
    bf16, f32, i32 = jnp.bfloat16, jnp.float32, jnp.int32
    hbm = pl.BlockSpec(memory_space=pltpu.HBM)
    vmem = pl.BlockSpec(memory_space=pltpu.VMEM)
    wide, narrow = (rows, columns), (rows, HEAD_DIM)
    dma = pltpu.SemaphoreType.DMA
    return pl.pallas_call(
        functools.partial(block_kernel, tokens, bits, nt),
        out_shape=(jax.ShapeDtypeStruct(wide, bf16), jax.ShapeDtypeStruct(narrow, bf16),
                   jax.ShapeDtypeStruct(narrow, bf16), jax.ShapeDtypeStruct((1, rows), f32)),
        in_specs=[pl.BlockSpec(memory_space=pltpu.SMEM)] + [hbm] * 11,
        out_specs=(vmem,) * 4,
        scratch_shapes=[
            pltpu.VMEM(wide, bf16), pltpu.VMEM(narrow, bf16), pltpu.VMEM(narrow, bf16), pltpu.VMEM(wide, bf16),
            pltpu.VMEM((rows, tiles * columns), bf16), pltpu.VMEM((rows, tiles * columns), bf16),
            pltpu.VMEM((HEAD_DIM, rows), bf16), pltpu.VMEM((rows, TILE), f32),
            pltpu.VMEM((rows, rows), bf16), pltpu.VMEM((1, rows), f32),
            pltpu.VMEM(narrow, f32), pltpu.VMEM(narrow, f32),
            pltpu.SMEM(caps.shape, f32),
            pltpu.VMEM((1, rows), i32), pltpu.VMEM((1, rows), i32), pltpu.VMEM((1, rows), i32),
            pltpu.VMEM((1, own), f32), pltpu.VMEM((1, own), f32), pltpu.VMEM((1, own), f32),
            pltpu.VMEM((1, 1, 128), f32), pltpu.VMEM((nt - 1, 1, 128), f32),
            pltpu.VMEM((1, 1, 128), f32), pltpu.VMEM((planes - 1, 1, 128), f32),
            pltpu.VMEM((1, 1, 128), f32), pltpu.VMEM((low, 1, 128), f32), pltpu.VMEM((1, 1, 128), f32),
            dma((6 + 2 * tiles,)), dma((3,)), dma((3,)), dma((3,)),
        ],
        compiler_params=pltpu.CompilerParams(
            collective_id=0, has_side_effects=True, vmem_limit_bytes=32 * 2**20),
        name="block",
    )(cnt, *in_hbm(logp_new.reshape(1, own), logp_old.reshape(1, own), advantage.reshape(1, own), caps,
                   seq_begin.reshape(1, rows), seg_begin.reshape(1, rows), version.reshape(1, rows), q, k, v, g))


def finish_kernel(coef, dq_in, dk_in, dv_in, dq_hbm, dk_hbm, dv_hbm, dq, sems):
    rows, columns = dq.shape
    tiles = rows // TILE
    passed = [pltpu.make_async_copy(dk_in, dk_hbm, sems.at[0]), pltpu.make_async_copy(dv_in, dv_hbm, sems.at[1])]
    stores = [pltpu.make_async_copy(dq.at[pl.ds(i * TILE, TILE)], dq_hbm.at[pl.ds(i * TILE, TILE)], sems.at[2 + i])
              for i in range(tiles)]
    for copy in passed:
        copy.start()
    for i in range(tiles):
        here = slice(i * TILE, (i + 1) * TILE)
        coef_col = jnp.broadcast_to(coef[:, here], (HEAD_DIM, TILE)).T
        for h in range(columns // HEAD_DIM):
            lanes = slice(h * HEAD_DIM, (h + 1) * HEAD_DIM)
            dq[here, lanes] = (dq_in[here, lanes].astype(jnp.float32) * coef_col).astype(dq.dtype)
        stores[i].start()
    for copy in stores + passed:
        copy.wait()


def finish(coef, dq, dk, dv):
    hbm = pl.BlockSpec(memory_space=pltpu.HBM)
    vmem = pl.BlockSpec(memory_space=pltpu.VMEM)
    return pl.pallas_call(
        finish_kernel,
        out_shape=tuple(jax.ShapeDtypeStruct(a.shape, a.dtype) for a in (dq, dk, dv)),
        in_specs=[vmem] * 4,
        out_specs=(hbm,) * 3,
        scratch_shapes=[pltpu.VMEM(dq.shape, dq.dtype), pltpu.SemaphoreType.DMA((2 + dq.shape[0] // TILE,))],
        compiler_params=pltpu.CompilerParams(vmem_limit_bytes=32 * 2**20),
        name="finish",
    )(coef, dq, dk, dv)


def solution(mesh):
    blocks, nt = mesh.shape["dp"], mesh.shape["tensor"]
    top = blocks.bit_length() - 1
    bits = (((0,), tuple(range(1, top))), ((0, top - 2, top - 1), tuple(range(1, top - 2))))

    def local(query_heads, key_heads, value_heads, logp_grad, logp_new, logp_old, advantage, ratio_caps,
              live_counts, seq_begin, seg_begin, policy_version):
        tokens = float(query_heads.shape[0] * blocks)
        dq, dk, dv, coef = block(tokens, bits, nt, live_counts, logp_new, logp_old, advantage, ratio_caps,
                                 seq_begin, seg_begin, policy_version, query_heads, key_heads, value_heads, logp_grad)
        return finish(coef, dq, dk, dv)

    row, every = P("dp"), P(("dp", "tensor"))
    both = P("dp", "tensor")
    return jax.shard_map(
        local,
        mesh=mesh,
        in_specs=(both, both, both, both, every, every, every, P(), row, row, row, row),
        out_specs=(both, both, both),
        check_vma=False,
    )
```
